32 devices in a mesh: leaf: 8 (over z, x), batch: 4 (over y, core).
Axes of the slice: x: 2, y: 2, z: 4, core: 2. Of those that a mesh axis runs over, the one named last changes fastest.
Arguments:
- pixels_low: int32 [80, 512], P('leaf', 'batch'), may hold values from 0 to 255
- pixels_mid: int32 [32, 512], P('leaf', 'batch'), may hold values from 0 to 255
- pixels_top: int32 [8, 512], P('leaf', 'batch'), may hold values from 0 to 255
- emit_low: bfloat16 [80, 256, 256], P('leaf'), may hold values from -153 to 0, as said below
- emit_mid: bfloat16 [32, 256, 256], P('leaf'), may hold values from -153 to 0, as said below
- emit_top: bfloat16 [8, 256, 256], P('leaf'), may hold values from -153 to 0, as said below
- trans_low: bfloat16 [80, 256, 256], P('leaf'), may hold values from 0.0001171875 to 3.515625, as said below
- trans_mid: bfloat16 [32, 256, 256], P('leaf'), may hold values from 0.0001171875 to 3.515625, as said below
- outside_top: float32 [8, 512, 256], P('leaf', 'batch'), may hold values from -1708 to -292, as said below
- parent_low: int32 [80], replicated, may hold values from 0 to 31, as said below
- parent_mid: int32 [32], replicated, may hold values from 0 to 7
Outputs:
- update_low: float32 [80, 256, 256], P('leaf', 'batch')
- update_mid: float32 [32, 256, 256], P('leaf', 'batch')
The draws below stay inside these ranges and needn't reach their ends.
Inputs may be any that keep to these rules, and one draw needn't show every extreme that they name: `emit_low`: Log-probabilities of pixel values given a state. `emit_mid`: Log-probabilities of pixel values given a state. `emit_top`: Log-probabilities of pixel values given a state. `trans_low`: positive edge weights. `trans_mid`: positive edge weights. `outside_top`: Log-likelihood of the rest of the image given a state. `parent_low`: among the 10 bottom-level nodes of one leaf index, at most 3 have a parent p held by another leaf index (leaf index p // 4); some leaf index has exactly 3.
All inputs are finite; a program needn't handle non-finite values.
Results may differ from the reference program's by a relative error of at most 0.0015.
Values sent between devices are 32-bit elements; how exact they have to be, the bound alone decides.
A program may use at most 64 MiB of HBM per device.

```python
import jax
import jax.numpy as jnp
from jax import lax

K = 256
V = 256
C0 = 10
C1 = 4
R0 = 3
B = 512
N0 = 80
N1 = 32
N2 = 8


def emission_draw(key, count):
    keys = jax.random.split(key, 2)
    base = jax.random.uniform(keys[0], (count, V, 1), jnp.float32, -9.0, -3.0)
    noise = jax.random.uniform(keys[1], (count, V, K), jnp.float32, -3.0, 3.0)
    return (base + noise).astype(jnp.bfloat16)


def transition_draw(key, count):
    keys = jax.random.split(key, 1)
    states = jnp.arange(K, dtype=jnp.int32)
    diagonal = (states[:, None] == states[None, :]).astype(jnp.float32)
    values = jnp.exp(jax.random.uniform(keys[0], (count, K, K), jnp.float32, -1.5, 1.5))
    return (values * (1.0 + 32.0 * diagonal) / K).astype(jnp.bfloat16)


def draw_emit_low(key, part):
    return emission_draw(jax.random.fold_in(key, 11), N0)


def draw_emit_mid(key, part):
    return emission_draw(jax.random.fold_in(key, 12), N1)


def draw_emit_top(key, part):
    return emission_draw(jax.random.fold_in(key, 13), N2)


def draw_trans_low(key, part):
    return transition_draw(jax.random.fold_in(key, 21), N0)


def draw_trans_mid(key, part):
    return transition_draw(jax.random.fold_in(key, 22), N1)


def draw_outside_top(key, part):
    keys = jax.random.split(jax.random.fold_in(key, 31), 2)
    offset = jax.random.uniform(keys[0], (N2, B, 1), jnp.float32, -1600.0, -400.0)
    detail = jax.random.uniform(keys[1], (N2, B, K), jnp.float32, -4.0, 4.0)
    return offset + detail


def draw_parent_low(key, part):
    devices = N0 // C0
    keys = jax.random.split(jax.random.fold_in(key, 41), 5)
    owners_now = jnp.arange(devices, dtype=jnp.int32)[:, None]
    counts = jax.random.randint(keys[0], (devices,), R0 - R0 // 2, R0 + 1)
    forced = jax.random.randint(keys[1], (), 0, devices)
    counts = jnp.where(jnp.arange(devices, dtype=jnp.int32) == forced, R0, counts)
    scores = jax.random.randint(keys[2], (devices, C0), 0, 1 << 20) * C0 + jnp.arange(C0, dtype=jnp.int32)[None, :]
    ranks = jnp.argsort(jnp.argsort(scores, axis=1), axis=1)
    remote = ranks < counts[:, None]
    hops = jax.random.randint(keys[3], (devices, C0), 1, devices)
    owners = jnp.where(remote, (owners_now + hops) % devices, owners_now)
    slots = jax.random.randint(keys[4], (devices, C0), 0, C1)
    return (owners * C1 + slots).reshape(N0).astype(jnp.int32)


def set_ends(values, key, low, largest):
    longest = values.shape.index(max(values.shape))
    spots = []
    for shift in (0, 1):
        where = [jax.random.randint(jax.random.fold_in(key, axis), (), 0, length) for axis, length in enumerate(values.shape)]
        where[longest] = (where[longest] + shift) % values.shape[longest]
        spots.append(tuple(where))
    return values.at[spots[0]].set(low).at[spots[1]].set(largest)


def setup_inputs(seed: int = 0) -> dict:
    streams_of = jax.random.split(jax.random.key(seed), 12)
    return {
        "pixels_low": set_ends(jax.random.randint(streams_of[0], (N0, B), 0, V), jax.random.fold_in(streams_of[0], 1), 0, V - 1).astype(jnp.int32),
        "pixels_mid": set_ends(jax.random.randint(streams_of[1], (N1, B), 0, V), jax.random.fold_in(streams_of[1], 1), 0, V - 1).astype(jnp.int32),
        "pixels_top": set_ends(jax.random.randint(streams_of[2], (N2, B), 0, V), jax.random.fold_in(streams_of[2], 1), 0, V - 1).astype(jnp.int32),
        "emit_low": draw_emit_low(jax.random.fold_in(streams_of[11], 71), 0),
        "emit_mid": draw_emit_mid(jax.random.fold_in(streams_of[11], 71), 0),
        "emit_top": draw_emit_top(jax.random.fold_in(streams_of[11], 71), 0),
        "trans_low": draw_trans_low(jax.random.fold_in(streams_of[11], 71), 0),
        "trans_mid": draw_trans_mid(jax.random.fold_in(streams_of[11], 71), 0),
        "outside_top": draw_outside_top(jax.random.fold_in(streams_of[11], 71), 0),
        "parent_low": draw_parent_low(jax.random.fold_in(streams_of[11], 71), 0),
        "parent_mid": set_ends(jax.random.randint(streams_of[10], (N1,), 0, N2), jax.random.fold_in(streams_of[10], 1), 0, N2 - 1).astype(jnp.int32),
    }


PSEUDO = 0.001


def lookup(table, pixels):
    return jnp.take(table, pixels, axis=0).astype(jnp.float32)


def upward(inside, weight):
    top = jnp.max(inside, axis=-1, keepdims=True)
    scaled = jnp.exp(inside - top).astype(jnp.bfloat16)
    linear = jnp.dot(scaled, weight.T, preferred_element_type=jnp.float32)
    return jnp.log(linear) + top, scaled


def edge_update(above, weight, scaled):
    peak = jnp.max(above, axis=-1, keepdims=True)
    pushed = jnp.exp(above - peak).astype(jnp.bfloat16)
    reach = jnp.dot(pushed, weight, preferred_element_type=jnp.float32)
    total = jnp.sum(reach * scaled.astype(jnp.float32), axis=-1, keepdims=True)
    share = (pushed.astype(jnp.float32) / total).astype(jnp.bfloat16)
    counts = jnp.dot(share.T, scaled, preferred_element_type=jnp.float32) * weight.astype(jnp.float32) + PSEUDO
    update = K * counts / jnp.sum(counts, axis=-1, keepdims=True)
    return update, jnp.log(reach) + peak


def reference(pixels_low, pixels_mid, pixels_top, emit_low, emit_mid, emit_top, trans_low, trans_mid, outside_top, parent_low, parent_mid):
    def low_up(sums, item):
        table, weight, pixels, parent = item
        up_low, scaled = upward(lookup(table, pixels), weight)
        return sums.at[parent].add(up_low), None

    sums_mid, ignored = lax.scan(low_up, jnp.zeros((N1, B, K), jnp.float32), (emit_low, trans_low, pixels_low, parent_low))
    inside_mid = jax.vmap(lookup)(emit_mid, pixels_mid) + sums_mid
    up_mid, scaled_mid = lax.map(lambda item: upward(item[0], item[1]), (inside_mid, trans_mid))
    sums_top = jax.ops.segment_sum(up_mid, parent_mid, num_segments=N2)
    total_top = jax.vmap(lookup)(emit_top, pixels_top) + sums_top + outside_top
    above_mid = total_top[parent_mid] - up_mid
    update_mid, outside_mid = lax.map(lambda item: edge_update(item[0], item[1], item[2]), (above_mid, trans_mid, scaled_mid))
    total_mid = inside_mid + outside_mid

    def low_down(item):
        table, weight, pixels, parent = item
        up_low, scaled = upward(lookup(table, pixels), weight)
        above = lax.dynamic_index_in_dim(total_mid, parent, 0, keepdims=False) - up_low
        update, unused = edge_update(above, weight, scaled)
        return update

    update_low = lax.map(low_down, (emit_low, trans_low, pixels_low, parent_low))
    return update_low, update_mid
```

```python
import functools

import jax
import jax.numpy as jnp
from jax import lax
from jax.experimental import pallas as pl
from jax.experimental.pallas import tpu as pltpu
from jax.sharding import PartitionSpec as P

PSEUDO = 0.001
REMOTE = 3
MESH = pl.DeviceIdType.MESH


def lookup_all(table, pixels):
    levels = jnp.arange(table.shape[1], dtype=jnp.int32)
    picks = (pixels[:, :, None] == levels[None, None, :]).astype(jnp.bfloat16)
    return jnp.einsum("nbv,nvk->nbk", picks, table, preferred_element_type=jnp.float32)


def upward_all(inside, weight):
    top = jnp.max(inside, axis=-1, keepdims=True)
    scaled = jnp.exp(inside - top).astype(jnp.bfloat16)
    linear = jnp.einsum("nbj,nij->nbi", scaled, weight, preferred_element_type=jnp.float32)
    return (jnp.log(linear) + top, scaled)


def edge_all(above, weight, scaled):
    peak = jnp.max(above, axis=-1, keepdims=True)
    pushed = jnp.exp(above - peak).astype(jnp.bfloat16)
    reach = jnp.einsum("nbi,nij->nbj", pushed, weight, preferred_element_type=jnp.float32)
    total = jnp.sum(reach * scaled.astype(jnp.float32), axis=-1, keepdims=True)
    share = (pushed.astype(jnp.float32) / total).astype(jnp.bfloat16)
    counts = jnp.einsum("nbi,nbj->nij", share, scaled, preferred_element_type=jnp.float32)
    return (counts * weight.astype(jnp.float32), jnp.log(reach) + peak)


def finish(summed):
    counts = summed + PSEUDO
    return counts.shape[-1] * counts / jnp.sum(counts, axis=-1, keepdims=True)


def body(
    pixels_low,
    pixels_mid,
    pixels_top,
    emit_low,
    emit_mid,
    emit_top,
    trans_low,
    trans_mid,
    outside_top,
    parent_low,
    parent_mid,
):
    devices = lax.axis_size("leaf")
    mid_count = emit_mid.shape[0]
    top_count = emit_top.shape[0]
    up_low, scaled_low = upward_all(lookup_all(emit_low, pixels_low), trans_low)
    emis_mid = lookup_all(emit_mid, pixels_mid)
    emis_top = lookup_all(emit_top, pixels_top)
    moved = lax.all_to_all(up_low, "leaf", split_axis=1, concat_axis=0, tiled=True)
    gathered_mid = jax.ops.segment_sum(moved, parent_low, num_segments=mid_count * devices)
    sums_mid = lax.all_to_all(gathered_mid, "leaf", split_axis=0, concat_axis=1, tiled=True)
    inside_mid = emis_mid + sums_mid
    up_mid, scaled_mid = upward_all(inside_mid, trans_mid)
    moved_mid = lax.all_to_all(up_mid, "leaf", split_axis=1, concat_axis=0, tiled=True)
    gathered_top = jax.ops.segment_sum(moved_mid, parent_mid, num_segments=top_count * devices)
    sums_top = lax.all_to_all(gathered_top, "leaf", split_axis=0, concat_axis=1, tiled=True)
    total_top = emis_top + sums_top + outside_top
    spread_top = lax.all_to_all(total_top, "leaf", split_axis=1, concat_axis=0, tiled=True)
    picked = lax.all_to_all(spread_top[parent_mid], "leaf", split_axis=0, concat_axis=1, tiled=True)
    counts_mid, outside_mid = edge_all(picked - up_mid, trans_mid, scaled_mid)
    update_mid = finish(lax.psum_scatter(counts_mid, "batch", scatter_dimension=1, tiled=True))
    total_mid = inside_mid + outside_mid
    spread_mid = lax.all_to_all(total_mid, "leaf", split_axis=1, concat_axis=0, tiled=True)
    above_low = lax.all_to_all(
        spread_mid[parent_low], "leaf", split_axis=0, concat_axis=1, tiled=True
    )
    counts_low, unused = edge_all(above_low - up_low, trans_low, scaled_low)
    update_low = finish(lax.psum_scatter(counts_low, "batch", scatter_dimension=1, tiled=True))
    return (update_low, update_mid)


def dot(a, b, left, right):
    return lax.dot_general(
        a, b, (((left,), (right,)), ((), ())), preferred_element_type=jnp.float32
    )


def kernel(
    leaves,
    parts,
    offsets,
    meta,
    pixels_low,
    pixels_mid,
    pixels_top,
    emit_low,
    emit_mid,
    emit_top,
    trans_low,
    trans_mid,
    outside_top,
    update_low,
    update_mid,
    pix,
    edge_top,
    own_top,
    far_up,
    far_slices,
    mid_send,
    mid_sums,
    scaled_low,
    linear_low,
    up_mid,
    up_slices,
    totals,
    total_send,
    total_mine,
    scaled_mid,
    linear_mid,
    post_mid,
    post_slices,
    post_send,
    post,
    counts_mid,
    counts_own,
    send_sem,
    recv_sem,
):
    at_parent_low, at_parent_mid, at_index, at_parent, at_place = offsets
    leaf = lax.axis_index("leaf")
    part = lax.axis_index("batch")
    devices = leaves * parts
    me = leaf * parts + part
    low_count = pixels_low.shape[0]
    mid_count = pixels_mid.shape[0]
    images = pixels_low.shape[1]
    states = trans_low.shape[2]
    share_rows = states // parts
    rows = states // devices

    def slice_of(l, q):
        return pl.ds(pl.multiple_of(q * share_rows + l * rows, rows), rows)

    def quarter_of(q):
        return pl.ds(pl.multiple_of(q * share_rows, share_rows), share_rows)

    def send(src, dst, phase, l, q):
        pltpu.make_async_remote_copy(
            src_ref=src,
            dst_ref=dst,
            send_sem=send_sem.at[phase],
            recv_sem=recv_sem.at[phase],
            device_id=(l, q),
            device_id_type=MESH,
        ).start()

    def wait_recv(ref, phase):
        pltpu.make_async_copy(ref, ref, recv_sem.at[phase]).wait()

    def wait_send(ref, phase):
        pltpu.make_async_copy(ref, ref, send_sem.at[phase]).wait()

    def each_other(step):
        def one(k, carry):
            t = lax.rem(me + k, devices)
            step(t, lax.div(t, parts), lax.rem(t, parts))
            return carry

        lax.fori_loop(1, devices, one, 0)

    def each_leaf(step):
        def one(k, carry):
            step(lax.rem(leaf + k, leaves))
            return carry

        lax.fori_loop(1, leaves, one, 0)

    def each_part(step):
        def one(k, carry):
            step(lax.rem(part + k, parts))
            return carry

        lax.fori_loop(1, parts, one, 0)

    barrier = pltpu.get_barrier_semaphore()

    def greet(t, l, q):
        pl.semaphore_signal(barrier, inc=1, device_id=(l, q), device_id_type=MESH)

    each_other(greet)

    levels = lax.broadcasted_iota(jnp.int32, (emit_low.shape[1], images), 0)

    def picks(row):
        return jnp.where(levels == row, 1.0, 0.0).astype(jnp.bfloat16)

    pix[part, 0:low_count, :] = pixels_low[...]
    pix[part, low_count : low_count + mid_count, :] = pixels_mid[...]
    own_top[...] = dot(emit_top[0], picks(pixels_top[...]), 0, 0) + outside_top[0].T
    pl.semaphore_wait(barrier, devices - 1)

    each_part(lambda q: send(pix.at[part], pix.at[part], 0, leaf, q))
    mine = pl.ds(pl.multiple_of(part * images, images), images)
    each_other(
        lambda t, l, q: send(
            own_top.at[slice_of(l, q)], edge_top.at[leaf, :, mine], 1, l, q
        )
    )
    edge_top[leaf, :, mine] = own_top[slice_of(leaf, part), :]
    wait_recv(pix.at[pl.ds(0, parts - 1)], 0)

    def lookup(table, node):
        chosen = jnp.concatenate(
            [picks(pix[q, pl.ds(node, 1), :]) for q in range(parts)], axis=1
        )
        return dot(table, chosen, 0, 0)

    def scale(inside):
        return jnp.exp(inside - jnp.max(inside, axis=0, keepdims=True))

    def far(s, carry):
        node = meta[at_index + leaf * REMOTE + s]
        scaled = scale(lookup(emit_low[node], node)).astype(jnp.bfloat16)
        far_up[s] = jnp.log(dot(trans_low[node], scaled, 1, 0))
        return carry

    lax.fori_loop(0, REMOTE, far, 0)
    each_leaf(
        lambda l: send(
            far_up.at[:, slice_of(l, part), :], far_slices.at[leaf], 2, l, part
        )
    )
    far_slices[leaf] = far_up[:, slice_of(leaf, part), :]

    total_mine[...] = lookup(emit_mid[part], low_count + part)

    def near(c, carry):
        scaled = scale(lookup(emit_low[c], c)).astype(jnp.bfloat16)
        scaled_low[c] = scaled
        linear = dot(trans_low[c], scaled, 1, 0)
        linear_mid[...] = linear
        linear_low[c] = linear_mid[quarter_of(part), :]
        weight = jnp.where(meta[at_parent_low + leaf * low_count + c] == me, 1.0, 0.0)
        total_mine[...] += weight * jnp.log(linear)
        return carry

    lax.fori_loop(0, low_count, near, 0)
    wait_recv(far_slices.at[pl.ds(0, leaves - 1)], 2)

    def sum_far(t):
        total = jnp.zeros(mid_send.shape[1:], jnp.float32)
        for l in range(leaves):
            for s in range(REMOTE):
                weight = jnp.where(meta[at_parent + l * REMOTE + s] == t, 1.0, 0.0)
                total += weight * far_slices[l, s]
        return total

    def send_sum(t, l, q):
        mid_send[t] = sum_far(t)
        send(mid_send.at[t], mid_sums.at[slice_of(leaf, part)], 3, l, q)

    each_other(send_sum)
    mid_sums[slice_of(leaf, part), :] = sum_far(me)
    wait_recv(mid_sums.at[pl.ds(0, states - rows)], 3)

    exact = scale(total_mine[...] + mid_sums[...])
    post_mid[...] = exact
    scaled_mid[...] = exact.astype(jnp.bfloat16)
    linear = dot(trans_mid[part], scaled_mid[...], 1, 0)
    linear_mid[...] = linear
    up_mid[...] = jnp.log(linear)
    each_other(lambda t, l, q: send(up_mid.at[slice_of(l, q)], up_slices.at[me], 4, l, q))
    up_slices[me] = up_mid[slice_of(leaf, part), :]
    wait_recv(own_top.at[pl.ds(0, states - rows)], 1)
    wait_recv(up_slices.at[pl.ds(0, devices - 1)], 4)

    def top(r, carry):
        total = edge_top[r]
        for p in range(devices):
            weight = jnp.where(meta[at_parent_mid + p] == r, 1.0, 0.0)
            total += weight * up_slices[p]
        totals[r] = total
        return carry

    lax.fori_loop(0, leaves, top, 0)

    def send_total(t, l, q):
        total_send[t] = totals[meta[at_parent_mid + t]]
        send(total_send.at[t], total_mine.at[slice_of(leaf, part)], 5, l, q)

    each_other(send_total)
    total_mine[slice_of(leaf, part), :] = totals[meta[at_parent_mid + me]]
    wait_recv(total_mine.at[pl.ds(0, states - rows)], 5)

    reached = scale(total_mine[...])
    share = (
        reached / (linear_mid[...] * jnp.sum(reached, axis=0, keepdims=True))
    ).astype(jnp.bfloat16)
    posterior = post_mid[...] * dot(trans_mid[part], share, 0, 0)
    post_mid[...] = posterior / jnp.sum(posterior, axis=0, keepdims=True)
    each_other(
        lambda t, l, q: send(post_mid.at[slice_of(l, q)], post_slices.at[me], 6, l, q)
    )
    each_part(lambda q: send(post_mid.at[quarter_of(q)], post.at[part], 7, leaf, q))
    post_slices[me] = post_mid[slice_of(leaf, part), :]
    post[part] = post_mid[quarter_of(part), :]

    def finished(share, scaled, weight):
        counts = dot(share, scaled, 1, 1) * weight.astype(jnp.float32) + PSEUDO
        return states * counts / jnp.sum(counts, axis=-1, keepdims=True)

    counts_own[...] = finished(share, scaled_mid[...], trans_mid[part])
    each_part(lambda q: send(counts_own.at[quarter_of(q)], counts_mid.at[part], 8, leaf, q))
    counts_mid[part] = counts_own[quarter_of(part), :]
    wait_recv(post_slices.at[pl.ds(0, devices - 1)], 6)

    def pick(l):
        for s in range(REMOTE):
            post_send[l, s] = post_slices[jnp.maximum(meta[at_parent + l * REMOTE + s], 0)]

    landing = pl.ds(pl.multiple_of(leaf * rows, rows), rows)

    def send_pick(l):
        pick(l)
        send(post_send.at[l], post.at[pl.ds(mid_count, REMOTE), landing], 9, l, part)

    each_leaf(send_pick)
    pick(leaf)
    post[mid_count : mid_count + REMOTE, landing, :] = post_send[leaf]
    wait_recv(post.at[pl.ds(0, parts - 1)], 7)
    wait_recv(post_send.at[pl.ds(0, leaves - 1)], 9)

    def low_update(c, carry):
        share = (post[meta[at_place + leaf * low_count + c]] / linear_low[c]).astype(
            jnp.bfloat16
        )
        update_low[c] = finished(share, scaled_low[c], trans_low[c, quarter_of(part), :])
        return carry

    lax.fori_loop(0, low_count, low_update, 0)
    wait_recv(counts_mid.at[pl.ds(0, parts - 1)], 8)
    update_mid[...] = counts_mid[...]

    wait_send(pix.at[pl.ds(0, parts - 1)], 0)
    wait_send(own_top.at[pl.ds(0, states - rows)], 1)
    wait_send(far_slices.at[pl.ds(0, leaves - 1)], 2)
    wait_send(mid_send.at[pl.ds(0, devices - 1)], 3)
    wait_send(up_slices.at[pl.ds(0, devices - 1)], 4)
    wait_send(total_send.at[pl.ds(0, devices - 1)], 5)
    wait_send(post_slices.at[pl.ds(0, devices - 1)], 6)
    wait_send(post.at[pl.ds(0, parts - 1)], 7)
    wait_send(counts_mid.at[pl.ds(0, parts - 1)], 8)
    wait_send(post_send.at[pl.ds(0, leaves - 1)], 9)


def plan(parent_low, parent_mid, leaves, low_count, mid_count):
    parents = parent_low.reshape(leaves, low_count)
    nodes = jnp.arange(low_count, dtype=jnp.int32)
    far = parents // mid_count != jnp.arange(leaves, dtype=jnp.int32)[:, None]
    before = far[:, None, :] & (nodes[None, :] < nodes[:, None])[None]
    rank = jnp.sum(before.astype(jnp.int32), axis=-1)
    slots = jnp.arange(REMOTE, dtype=jnp.int32)[None, :, None]
    chosen = far[:, None, :] & (rank[:, None, :] == slots)
    index = jnp.sum(jnp.where(chosen, nodes, 0), axis=-1)
    parent = jnp.sum(jnp.where(chosen, parents[:, None, :] + 1, 0), axis=-1) - 1
    place = jnp.where(far, mid_count + rank, parents % mid_count)
    pieces = [parent_low, parent_mid, index.reshape(-1), parent.reshape(-1), place.reshape(-1)]
    offsets = [0]
    for piece in pieces[:-1]:
        offsets.append(offsets[-1] + piece.shape[0])
    return jnp.concatenate(pieces), tuple(offsets)


def fused(
    leaves,
    parts,
    pixels_low,
    pixels_mid,
    pixels_top,
    emit_low,
    emit_mid,
    emit_top,
    trans_low,
    trans_mid,
    outside_top,
    parent_low,
    parent_mid,
):
    low_count, images = pixels_low.shape
    mid_count = pixels_mid.shape[0]
    states = trans_low.shape[2]
    devices = leaves * parts
    share_rows = states // parts
    rows = states // devices
    whole = images * parts
    meta, offsets = plan(parent_low, parent_mid, leaves, low_count, mid_count)
    held = -(-(low_count + mid_count) // 8) * 8
    real = jnp.float32
    return pl.pallas_call(
        functools.partial(kernel, leaves, parts, offsets),
        out_shape=(
            jax.ShapeDtypeStruct((low_count, share_rows, states), real),
            jax.ShapeDtypeStruct((mid_count, share_rows, states), real),
        ),
        in_specs=[pl.BlockSpec(memory_space=pltpu.SMEM)]
        + [pl.BlockSpec(memory_space=pltpu.VMEM)] * 9,
        out_specs=(pl.BlockSpec(memory_space=pltpu.VMEM),) * 2,
        scratch_shapes=[
            pltpu.VMEM((parts, held, images), jnp.int32),
            pltpu.VMEM((leaves, rows, whole), real),
            pltpu.VMEM((states, images), real),
            pltpu.VMEM((REMOTE, states, whole), real),
            pltpu.VMEM((leaves, REMOTE, rows, whole), real),
            pltpu.VMEM((devices, rows, whole), real),
            pltpu.VMEM((states, whole), real),
            pltpu.VMEM((low_count, states, whole), jnp.bfloat16),
            pltpu.VMEM((low_count, share_rows, whole), real),
            pltpu.VMEM((states, whole), real),
            pltpu.VMEM((devices, rows, whole), real),
            pltpu.VMEM((leaves, rows, whole), real),
            pltpu.VMEM((devices, rows, whole), real),
            pltpu.VMEM((states, whole), real),
            pltpu.VMEM((states, whole), jnp.bfloat16),
            pltpu.VMEM((states, whole), real),
            pltpu.VMEM((states, whole), real),
            pltpu.VMEM((devices, rows, whole), real),
            pltpu.VMEM((leaves, REMOTE, rows, whole), real),
            pltpu.VMEM((mid_count + REMOTE, share_rows, whole), real),
            pltpu.VMEM((mid_count, share_rows, states), real),
            pltpu.VMEM((states, states), real),
            pltpu.SemaphoreType.DMA((10,)),
            pltpu.SemaphoreType.DMA((10,)),
        ],
        compiler_params=pltpu.CompilerParams(
            collective_id=0, has_side_effects=True, vmem_limit_bytes=48 * 2**20
        ),
    )(
        meta,
        pixels_low,
        pixels_mid,
        pixels_top,
        emit_low,
        emit_mid,
        emit_top,
        trans_low,
        trans_mid,
        outside_top,
    )


def solution(mesh):
    leaves, parts = mesh.shape["leaf"], mesh.shape["batch"]
    fits = 256 % (8 * leaves * parts) == 0
    chosen = functools.partial(fused, leaves, parts) if fits else body
    return jax.shard_map(
        chosen,
        mesh=mesh,
        in_specs=(
            P("leaf", "batch"),
            P("leaf", "batch"),
            P("leaf", "batch"),
            P("leaf", None, None),
            P("leaf", None, None),
            P("leaf", None, None),
            P("leaf", None, None),
            P("leaf", None, None),
            P("leaf", "batch", None),
            P(),
            P(),
        ),
        out_specs=(P("leaf", "batch", None), P("leaf", "batch", None)),
        check_vma=False,
    )
```

```python
import functools

import jax
import jax.numpy as jnp
from jax import lax
from jax.experimental import pallas as pl
from jax.experimental.pallas import tpu as pltpu
from jax.sharding import PartitionSpec as P

PSEUDO = 0.001
REMOTE = 3
HALVES = 1
STRIDE = 13
MESH = pl.DeviceIdType.MESH


def lookup_all(table, pixels):
    levels = jnp.arange(table.shape[1], dtype=jnp.int32)
    picks = (pixels[:, :, None] == levels[None, None, :]).astype(jnp.bfloat16)
    return jnp.einsum("nbv,nvk->nbk", picks, table, preferred_element_type=jnp.float32)


def upward_all(inside, weight):
    top = jnp.max(inside, axis=-1, keepdims=True)
    scaled = jnp.exp(inside - top).astype(jnp.bfloat16)
    linear = jnp.einsum("nbj,nij->nbi", scaled, weight, preferred_element_type=jnp.float32)
    return (jnp.log(linear) + top, scaled)


def edge_all(above, weight, scaled):
    peak = jnp.max(above, axis=-1, keepdims=True)
    pushed = jnp.exp(above - peak).astype(jnp.bfloat16)
    reach = jnp.einsum("nbi,nij->nbj", pushed, weight, preferred_element_type=jnp.float32)
    total = jnp.sum(reach * scaled.astype(jnp.float32), axis=-1, keepdims=True)
    share = (pushed.astype(jnp.float32) / total).astype(jnp.bfloat16)
    counts = jnp.einsum("nbi,nbj->nij", share, scaled, preferred_element_type=jnp.float32)
    return (counts * weight.astype(jnp.float32), jnp.log(reach) + peak)


def finish(summed):
    counts = summed + PSEUDO
    return counts.shape[-1] * counts / jnp.sum(counts, axis=-1, keepdims=True)


def body(
    pixels_low,
    pixels_mid,
    pixels_top,
    emit_low,
    emit_mid,
    emit_top,
    trans_low,
    trans_mid,
    outside_top,
    parent_low,
    parent_mid,
):
    devices = lax.axis_size("leaf")
    mid_count = emit_mid.shape[0]
    top_count = emit_top.shape[0]
    up_low, scaled_low = upward_all(lookup_all(emit_low, pixels_low), trans_low)
    emis_mid = lookup_all(emit_mid, pixels_mid)
    emis_top = lookup_all(emit_top, pixels_top)
    moved = lax.all_to_all(up_low, "leaf", split_axis=1, concat_axis=0, tiled=True)
    gathered_mid = jax.ops.segment_sum(moved, parent_low, num_segments=mid_count * devices)
    sums_mid = lax.all_to_all(gathered_mid, "leaf", split_axis=0, concat_axis=1, tiled=True)
    inside_mid = emis_mid + sums_mid
    up_mid, scaled_mid = upward_all(inside_mid, trans_mid)
    moved_mid = lax.all_to_all(up_mid, "leaf", split_axis=1, concat_axis=0, tiled=True)
    gathered_top = jax.ops.segment_sum(moved_mid, parent_mid, num_segments=top_count * devices)
    sums_top = lax.all_to_all(gathered_top, "leaf", split_axis=0, concat_axis=1, tiled=True)
    total_top = emis_top + sums_top + outside_top
    spread_top = lax.all_to_all(total_top, "leaf", split_axis=1, concat_axis=0, tiled=True)
    picked = lax.all_to_all(spread_top[parent_mid], "leaf", split_axis=0, concat_axis=1, tiled=True)
    counts_mid, outside_mid = edge_all(picked - up_mid, trans_mid, scaled_mid)
    update_mid = finish(lax.psum_scatter(counts_mid, "batch", scatter_dimension=1, tiled=True))
    total_mid = inside_mid + outside_mid
    spread_mid = lax.all_to_all(total_mid, "leaf", split_axis=1, concat_axis=0, tiled=True)
    above_low = lax.all_to_all(
        spread_mid[parent_low], "leaf", split_axis=0, concat_axis=1, tiled=True
    )
    counts_low, unused = edge_all(above_low - up_low, trans_low, scaled_low)
    update_low = finish(lax.psum_scatter(counts_low, "batch", scatter_dimension=1, tiled=True))
    return (update_low, update_mid)


def dot(a, b, left, right):
    return lax.dot_general(
        a, b, (((left,), (right,)), ((), ())), preferred_element_type=jnp.float32
    )


def kernel(
    leaves,
    parts,
    parent_low,
    parent_mid,
    pixels_low_hbm,
    pixels_mid_hbm,
    pixels_top_hbm,
    emit_low_hbm,
    emit_mid_hbm,
    emit_top_hbm,
    trans_low_hbm,
    trans_mid_hbm,
    outside_top_hbm,
    update_low,
    update_mid,
    far_index,
    far_parent,
    place,
    pixels_low,
    pixels_mid,
    pixels_top,
    emit_low,
    emit_mid,
    emit_top,
    trans_low,
    trans_mid,
    outside_top,
    pix,
    edge_top,
    own_top,
    far_up,
    far_slices,
    mid_send,
    mid_sums,
    inside_own,
    scaled_low,
    linear_low,
    linear_full,
    up_mid,
    up_slices,
    totals,
    total_send,
    total_mine,
    scaled_mid,
    linear_mid,
    share_mid,
    post_mid,
    post_slices,
    post_send,
    post_near,
    post_far,
    counts_mid,
    counts_own,
    far_counts,
    send_sem,
    recv_sem,
    load_sem,
):
    leaf = lax.axis_index("leaf")
    part = lax.axis_index("batch")
    devices = leaves * parts
    me = leaf * parts + part
    low_count = pixels_low.shape[0]
    mid_count = pixels_mid.shape[0]
    images = pixels_low.shape[1]
    states = trans_low.shape[2]
    share_rows = states // parts
    rows = states // devices
    wide = images * parts // HALVES

    loads = [
        pltpu.make_async_copy(source, target, load_sem.at[i])
        for i, (source, target) in enumerate(
            (
                (pixels_low_hbm, pixels_low),
                (pixels_mid_hbm, pixels_mid),
                (pixels_top_hbm, pixels_top),
                (emit_top_hbm, emit_top),
                (outside_top_hbm, outside_top),
                (emit_low_hbm, emit_low),
                (trans_low_hbm, trans_low),
                (emit_mid_hbm.at[part], emit_mid),
                (trans_mid_hbm.at[part], trans_mid),
            )
        )
    ]
    for load in loads:
        load.start()

    def slice_of(l, q):
        return pl.ds(pl.multiple_of(q * share_rows + l * rows, rows), rows)

    def quarter_of(q):
        return pl.ds(pl.multiple_of(q * share_rows, share_rows), share_rows)

    def lanes(h):
        return pl.ds(h * wide, wide)

    def send(src, dst, phase, l, q):
        pltpu.make_async_remote_copy(
            src_ref=src,
            dst_ref=dst,
            send_sem=send_sem.at[phase],
            recv_sem=recv_sem.at[phase],
            device_id=(l, q),
            device_id_type=MESH,
        ).start()

    def wait_recv(ref, phase):
        pltpu.make_async_copy(ref, ref, recv_sem.at[phase]).wait()

    def wait_send(ref, phase):
        pltpu.make_async_copy(ref, ref, send_sem.at[phase]).wait()

    def each_other(step):
        def one(k, carry):
            t = lax.rem(me + STRIDE * k, devices)
            step(t, lax.div(t, parts), lax.rem(t, parts))
            return carry

        lax.fori_loop(1, devices, one, 0)

    def each_leaf(step):
        def one(k, carry):
            step(lax.rem(leaf + 3 * k, leaves))
            return carry

        lax.fori_loop(1, leaves, one, 0)

    def each_part(step):
        def one(k, carry):
            step(lax.rem(part + k, parts))
            return carry

        lax.fori_loop(1, parts, one, 0)

    barrier = pltpu.get_barrier_semaphore()

    def greet(t, l, q):
        pl.semaphore_signal(barrier, inc=1, device_id=(l, q), device_id_type=MESH)

    each_other(greet)

    def far_row(l, carry):
        found = jnp.int32(0)
        parents = [jnp.int32(-1)] * REMOTE
        for c in range(low_count):
            parent = parent_low[l * low_count + c]
            away = lax.div(parent, mid_count) != l
            for s in range(REMOTE):
                parents[s] = jnp.where(away & (found == s), parent, parents[s])
            found = found + jnp.where(away, 1, 0)
        for s in range(REMOTE):
            far_parent[l * REMOTE + s] = parents[s]
        return carry

    lax.fori_loop(0, leaves, far_row, 0)
    found = jnp.int32(0)
    nodes = [jnp.int32(0)] * REMOTE
    for c in range(low_count):
        parent = parent_low[leaf * low_count + c]
        away = lax.div(parent, mid_count) != leaf
        for s in range(REMOTE):
            nodes[s] = jnp.where(away & (found == s), c, nodes[s])
        place[c] = jnp.where(
            away, mid_count + jnp.minimum(found, REMOTE - 1), lax.rem(parent, mid_count)
        )
        found = found + jnp.where(away, 1, 0)
    for s in range(REMOTE):
        far_index[s] = nodes[s]

    levels = lax.broadcasted_iota(jnp.int32, (emit_low.shape[1], images), 0)

    def picks(row):
        return jnp.where(levels == row, 1.0, 0.0).astype(jnp.bfloat16)

    loads[0].wait()
    loads[1].wait()
    pix[part, 0:low_count, :] = pixels_low[...]
    pix[part, low_count : low_count + mid_count, :] = pixels_mid[...]
    pl.semaphore_wait(barrier, devices - 1)
    each_part(lambda q: send(pix.at[part], pix.at[part], 0, leaf, q))
    for load in loads[2:5]:
        load.wait()
    own_top[...] = dot(emit_top[0], picks(pixels_top[...]), 0, 0) + outside_top[0].T
    mine = pl.ds(pl.multiple_of(part * images, images), images)
    each_other(
        lambda t, l, q: send(
            own_top.at[slice_of(l, q)], edge_top.at[leaf, :, mine], 1, l, q
        )
    )
    edge_top[leaf, :, mine] = own_top[slice_of(leaf, part), :]
    loads[5].wait()
    loads[6].wait()
    wait_recv(pix.at[pl.ds(0, parts - 1)], 0)

    def lookup(table, node, first, last):
        chosen = jnp.concatenate(
            [picks(pix[q, pl.ds(node, 1), :]) for q in range(first, last)], axis=1
        )
        return dot(table, chosen, 0, 0)

    def scale(inside):
        return jnp.exp(inside - jnp.max(inside, axis=0, keepdims=True))

    per = parts // HALVES
    for h in range(HALVES):

        def far(s, carry):
            node = far_index[s]
            scaled = scale(lookup(emit_low[node], node, h * per, h * per + per))
            far_up[h, s] = jnp.log(dot(trans_low[node], scaled.astype(jnp.bfloat16), 1, 0))
            return carry

        lax.fori_loop(0, REMOTE, far, 0)
        each_leaf(
            lambda l: send(
                far_up.at[h, :, slice_of(l, part), :],
                far_slices.at[h, leaf],
                10 + h,
                l,
                part,
            )
        )
        far_slices[h, leaf] = far_up[h, :, slice_of(leaf, part), :]

    loads[7].wait()
    loads[8].wait()
    inside_own[...] = lookup(emit_mid[...], low_count + part, 0, parts)

    def near(c, carry):
        scaled = scale(lookup(emit_low[c], c, 0, parts)).astype(jnp.bfloat16)
        scaled_low[c] = scaled
        linear = dot(trans_low[c], scaled, 1, 0)
        linear_full[...] = linear
        linear_low[c] = linear_full[quarter_of(part), :]
        weight = jnp.where(parent_low[leaf * low_count + c] == me, 1.0, 0.0)
        inside_own[...] += weight * jnp.log(linear)
        return carry

    lax.fori_loop(0, low_count // 2, near, 0)

    for h in range(HALVES):
        wait_recv(far_slices.at[h, pl.ds(0, leaves - 1)], 10 + h)

        def sum_far(t):
            total = jnp.zeros((rows, wide), jnp.float32)
            for l in range(leaves):
                for s in range(REMOTE):
                    weight = jnp.where(far_parent[l * REMOTE + s] == t, 1.0, 0.0)
                    total += weight * far_slices[h, l, s]
            return total

        def send_sum(t, l, q):
            mid_send[h, t] = sum_far(t)
            send(mid_send.at[h, t], mid_sums.at[h, slice_of(leaf, part)], 12 + h, l, q)

        each_other(send_sum)
        mid_sums[h, slice_of(leaf, part), :] = sum_far(me)

    lax.fori_loop(low_count // 2, low_count, near, 0)

    for h in range(HALVES):
        wait_recv(mid_sums.at[h, pl.ds(0, states - rows)], 12 + h)
        exact = scale(inside_own[:, lanes(h)] + mid_sums[h])
        post_mid[h] = exact
        scaled = exact.astype(jnp.bfloat16)
        scaled_mid[:, lanes(h)] = scaled
        linear = dot(trans_mid[...], scaled, 1, 0)
        linear_mid[h] = linear
        up_mid[h] = jnp.log(linear)
        each_other(
            lambda t, l, q: send(
                up_mid.at[h, slice_of(l, q)], up_slices.at[h, me], 14 + h, l, q
            )
        )
        up_slices[h, me] = up_mid[h, slice_of(leaf, part), :]

    wait_recv(own_top.at[pl.ds(0, states - rows)], 1)
    for h in range(HALVES):
        wait_recv(up_slices.at[h, pl.ds(0, devices - 1)], 14 + h)

        def top(r, carry):
            total = edge_top[r, :, lanes(h)]
            for p in range(devices):
                weight = jnp.where(parent_mid[p] == r, 1.0, 0.0)
                total += weight * up_slices[h, p]
            totals[h, r] = total
            return carry

        lax.fori_loop(0, leaves, top, 0)

        def send_total(t, l, q):
            total_send[h, t] = totals[h, parent_mid[t]]
            send(total_send.at[h, t], total_mine.at[h, slice_of(leaf, part)], 16 + h, l, q)

        each_other(send_total)
        total_mine[h, slice_of(leaf, part), :] = totals[h, parent_mid[me]]

    for h in range(HALVES):
        wait_recv(total_mine.at[h, pl.ds(0, states - rows)], 16 + h)
        reached = scale(total_mine[h])
        share = (
            reached / (linear_mid[h] * jnp.sum(reached, axis=0, keepdims=True))
        ).astype(jnp.bfloat16)
        share_mid[:, lanes(h)] = share
        posterior = post_mid[h] * dot(trans_mid[...], share, 0, 0)
        post_mid[h] = posterior / jnp.sum(posterior, axis=0, keepdims=True)
        each_other(
            lambda t, l, q: send(
                post_mid.at[h, slice_of(l, q)], post_slices[h].at[me], 18 + h, l, q
            )
        )
        post_slices[h][me] = post_mid[h, slice_of(leaf, part), :]
        each_part(
            lambda q: send(
                post_mid.at[h, quarter_of(q)], post_near.at[part, :, lanes(h)], 20 + h, leaf, q
            )
        )
        post_near[part, :, lanes(h)] = post_mid[h, quarter_of(part), :]

    def finished(share, scaled, weight):
        counts = dot(share, scaled, 1, 1) * weight.astype(jnp.float32) + PSEUDO
        return states * counts / jnp.sum(counts, axis=-1, keepdims=True)

    counts_own[...] = finished(share_mid[...], scaled_mid[...], trans_mid[...])
    each_part(lambda q: send(counts_own.at[quarter_of(q)], counts_mid.at[part], 2, leaf, q))
    counts_mid[part] = counts_own[quarter_of(part), :]

    landing = pl.ds(pl.multiple_of(leaf * rows, rows), rows)
    for h in range(HALVES):
        wait_recv(post_slices[h].at[pl.ds(0, devices - 1)], 18 + h)

        def pick(l):
            for s in range(REMOTE):
                parent = jnp.maximum(far_parent[l * REMOTE + s], 0)
                post_send[h, l, s] = post_slices[h][parent]

        def send_pick(l):
            pick(l)
            send(
                post_send.at[h, l],
                post_far.at[:, landing, lanes(h)],
                22 + h,
                l,
                part,
            )

        each_leaf(send_pick)
        pick(leaf)
        post_far[:, landing, lanes(h)] = post_send[h, leaf]

    def update_of(c, found):
        share = (found / linear_low[c]).astype(jnp.bfloat16)
        return finished(share, scaled_low[c], trans_low[c, quarter_of(part), :])

    for h in range(HALVES):
        wait_recv(post_mid.at[h, pl.ds(0, states - share_rows)], 20 + h)

    def near_update(c, carry):
        update_low[c] = update_of(c, post_near[jnp.minimum(place[c], mid_count - 1)])
        return carry

    lax.fori_loop(0, low_count, near_update, 0)
    wait_recv(counts_mid.at[pl.ds(0, parts - 1)], 2)
    update_mid[...] = counts_mid[...]
    for h in range(HALVES):
        wait_recv(post_send.at[h, pl.ds(0, leaves - 1)], 22 + h)

    def far_update(s, carry):
        far_counts[s] = update_of(far_index[s], post_far[s])
        return carry

    lax.fori_loop(0, REMOTE, far_update, 0)

    def choose(c, carry):
        slot = place[c] - mid_count
        update_low[c] = jnp.where(
            slot >= 0, far_counts[jnp.maximum(slot, 0)], update_low[c]
        )
        return carry

    lax.fori_loop(0, low_count, choose, 0)

    wait_send(pix.at[pl.ds(0, parts - 1)], 0)
    wait_send(own_top.at[pl.ds(0, states - rows)], 1)
    wait_send(counts_mid.at[pl.ds(0, parts - 1)], 2)
    for h in range(HALVES):
        wait_send(far_slices.at[h, pl.ds(0, leaves - 1)], 10 + h)
        wait_send(mid_send.at[h, pl.ds(0, devices - 1)], 12 + h)
        wait_send(up_slices.at[h, pl.ds(0, devices - 1)], 14 + h)
        wait_send(total_send.at[h, pl.ds(0, devices - 1)], 16 + h)
        wait_send(post_slices[h].at[pl.ds(0, devices - 1)], 18 + h)
        wait_send(post_mid.at[h, pl.ds(0, states - share_rows)], 20 + h)
        wait_send(post_send.at[h, pl.ds(0, leaves - 1)], 22 + h)


def fused(
    leaves,
    parts,
    pixels_low,
    pixels_mid,
    pixels_top,
    emit_low,
    emit_mid,
    emit_top,
    trans_low,
    trans_mid,
    outside_top,
    parent_low,
    parent_mid,
):
    low_count, images = pixels_low.shape
    mid_count = pixels_mid.shape[0]
    states = trans_low.shape[2]
    devices = leaves * parts
    share_rows = states // parts
    rows = states // devices
    whole = images * parts
    wide = whole // HALVES
    held = -(-(low_count + mid_count) // 8) * 8
    real, half = jnp.float32, jnp.bfloat16
    vmem = pltpu.VMEM
    arrays = (pixels_low, pixels_mid, pixels_top, emit_low, emit_mid, emit_top, trans_low)
    arrays += (trans_mid, outside_top)
    return pl.pallas_call(
        functools.partial(kernel, leaves, parts),
        out_shape=(
            jax.ShapeDtypeStruct((low_count, share_rows, states), real),
            jax.ShapeDtypeStruct((mid_count, share_rows, states), real),
        ),
        in_specs=[pl.BlockSpec(memory_space=pltpu.SMEM)] * 2
        + [pl.BlockSpec(memory_space=pltpu.HBM)] * len(arrays),
        out_specs=(pl.BlockSpec(memory_space=pltpu.VMEM),) * 2,
        scratch_shapes=[
            pltpu.SMEM((REMOTE,), jnp.int32),
            pltpu.SMEM((leaves * REMOTE,), jnp.int32),
            pltpu.SMEM((low_count,), jnp.int32),
            vmem(pixels_low.shape, jnp.int32),
            vmem(pixels_mid.shape, jnp.int32),
            vmem(pixels_top.shape, jnp.int32),
            vmem(emit_low.shape, half),
            vmem(emit_mid.shape[1:], half),
            vmem(emit_top.shape, half),
            vmem(trans_low.shape, half),
            vmem(trans_mid.shape[1:], half),
            vmem(outside_top.shape, real),
            vmem((parts, held, images), jnp.int32),
            vmem((leaves, rows, whole), real),
            vmem((states, images), real),
            vmem((HALVES, REMOTE, states, wide), real),
            vmem((HALVES, leaves, REMOTE, rows, wide), real),
            vmem((HALVES, devices, rows, wide), real),
            vmem((HALVES, states, wide), real),
            vmem((states, whole), real),
            vmem((low_count, states, whole), half),
            vmem((low_count, share_rows, whole), real),
            vmem((states, whole), real),
            vmem((HALVES, states, wide), real),
            vmem((HALVES, devices, rows, wide), real),
            vmem((HALVES, leaves, rows, wide), real),
            vmem((HALVES, devices, rows, wide), real),
            vmem((HALVES, states, wide), real),
            vmem((states, whole), half),
            vmem((HALVES, states, wide), real),
            vmem((states, whole), half),
            vmem((HALVES, states, wide), real),
            (vmem((devices, rows, wide), real),) * HALVES,
            vmem((HALVES, leaves, REMOTE, rows, wide), real),
            vmem((mid_count, share_rows, whole), real),
            vmem((REMOTE, share_rows, whole), real),
            vmem((mid_count, share_rows, states), real),
            vmem((states, states), real),
            vmem((REMOTE, share_rows, states), real),
            pltpu.SemaphoreType.DMA((24,)),
            pltpu.SemaphoreType.DMA((24,)),
            pltpu.SemaphoreType.DMA((len(arrays),)),
        ],
        compiler_params=pltpu.CompilerParams(
            collective_id=0, has_side_effects=True, vmem_limit_bytes=48 * 2**20
        ),
    )(parent_low, parent_mid, *arrays)


def solution(mesh):
    leaves, parts = mesh.shape["leaf"], mesh.shape["batch"]
    fits = 256 % (8 * leaves * parts) == 0
    chosen = functools.partial(fused, leaves, parts) if fits else body
    return jax.shard_map(
        chosen,
        mesh=mesh,
        in_specs=(
            P("leaf", "batch"),
            P("leaf", "batch"),
            P("leaf", "batch"),
            P("leaf", None, None),
            P("leaf", None, None),
            P("leaf", None, None),
            P("leaf", None, None),
            P("leaf", None, None),
            P("leaf", "batch", None),
            P(),
            P(),
        ),
        out_specs=(P("leaf", "batch", None), P("leaf", "batch", None)),
        check_vma=False,
    )
```

```python
import functools

import jax
import jax.numpy as jnp
from jax import lax
from jax.experimental import pallas as pl
from jax.experimental.pallas import tpu as pltpu
from jax.sharding import PartitionSpec as P

PSEUDO = 0.001
REMOTE = 3
HALVES = 2
STRIDE = 13
MESH = pl.DeviceIdType.MESH


def lookup_all(table, pixels):
    levels = jnp.arange(table.shape[1], dtype=jnp.int32)
    picks = (pixels[:, :, None] == levels[None, None, :]).astype(jnp.bfloat16)
    return jnp.einsum("nbv,nvk->nbk", picks, table, preferred_element_type=jnp.float32)


def upward_all(inside, weight):
    top = jnp.max(inside, axis=-1, keepdims=True)
    scaled = jnp.exp(inside - top).astype(jnp.bfloat16)
    linear = jnp.einsum("nbj,nij->nbi", scaled, weight, preferred_element_type=jnp.float32)
    return (jnp.log(linear) + top, scaled)


def edge_all(above, weight, scaled):
    peak = jnp.max(above, axis=-1, keepdims=True)
    pushed = jnp.exp(above - peak).astype(jnp.bfloat16)
    reach = jnp.einsum("nbi,nij->nbj", pushed, weight, preferred_element_type=jnp.float32)
    total = jnp.sum(reach * scaled.astype(jnp.float32), axis=-1, keepdims=True)
    share = (pushed.astype(jnp.float32) / total).astype(jnp.bfloat16)
    counts = jnp.einsum("nbi,nbj->nij", share, scaled, preferred_element_type=jnp.float32)
    return (counts * weight.astype(jnp.float32), jnp.log(reach) + peak)


def finish(summed):
    counts = summed + PSEUDO
    return counts.shape[-1] * counts / jnp.sum(counts, axis=-1, keepdims=True)


def body(
    pixels_low,
    pixels_mid,
    pixels_top,
    emit_low,
    emit_mid,
    emit_top,
    trans_low,
    trans_mid,
    outside_top,
    parent_low,
    parent_mid,
):
    devices = lax.axis_size("leaf")
    mid_count = emit_mid.shape[0]
    top_count = emit_top.shape[0]
    up_low, scaled_low = upward_all(lookup_all(emit_low, pixels_low), trans_low)
    emis_mid = lookup_all(emit_mid, pixels_mid)
    emis_top = lookup_all(emit_top, pixels_top)
    moved = lax.all_to_all(up_low, "leaf", split_axis=1, concat_axis=0, tiled=True)
    gathered_mid = jax.ops.segment_sum(moved, parent_low, num_segments=mid_count * devices)
    sums_mid = lax.all_to_all(gathered_mid, "leaf", split_axis=0, concat_axis=1, tiled=True)
    inside_mid = emis_mid + sums_mid
    up_mid, scaled_mid = upward_all(inside_mid, trans_mid)
    moved_mid = lax.all_to_all(up_mid, "leaf", split_axis=1, concat_axis=0, tiled=True)
    gathered_top = jax.ops.segment_sum(moved_mid, parent_mid, num_segments=top_count * devices)
    sums_top = lax.all_to_all(gathered_top, "leaf", split_axis=0, concat_axis=1, tiled=True)
    total_top = emis_top + sums_top + outside_top
    spread_top = lax.all_to_all(total_top, "leaf", split_axis=1, concat_axis=0, tiled=True)
    picked = lax.all_to_all(spread_top[parent_mid], "leaf", split_axis=0, concat_axis=1, tiled=True)
    counts_mid, outside_mid = edge_all(picked - up_mid, trans_mid, scaled_mid)
    update_mid = finish(lax.psum_scatter(counts_mid, "batch", scatter_dimension=1, tiled=True))
    total_mid = inside_mid + outside_mid
    spread_mid = lax.all_to_all(total_mid, "leaf", split_axis=1, concat_axis=0, tiled=True)
    above_low = lax.all_to_all(
        spread_mid[parent_low], "leaf", split_axis=0, concat_axis=1, tiled=True
    )
    counts_low, unused = edge_all(above_low - up_low, trans_low, scaled_low)
    update_low = finish(lax.psum_scatter(counts_low, "batch", scatter_dimension=1, tiled=True))
    return (update_low, update_mid)


def dot(a, b, left, right):
    return lax.dot_general(
        a, b, (((left,), (right,)), ((), ())), preferred_element_type=jnp.float32
    )


def kernel(
    leaves,
    parts,
    parent_low,
    parent_mid,
    pixels_low_hbm,
    pixels_mid_hbm,
    pixels_top_hbm,
    emit_low_hbm,
    emit_mid_hbm,
    emit_top_hbm,
    trans_low_hbm,
    trans_mid_hbm,
    outside_top_hbm,
    update_low,
    update_mid,
    far_index,
    far_parent,
    place,
    pixels_low,
    pixels_mid,
    pixels_top,
    emit_low,
    emit_mid,
    emit_top,
    trans_low,
    trans_mid,
    outside_top,
    pix,
    edge_top,
    own_top,
    far_up,
    far_slices,
    mid_send,
    mid_sums,
    inside_own,
    scaled_low,
    linear_low,
    linear_full,
    up_mid,
    up_slices,
    totals,
    total_send,
    total_mine,
    scaled_mid,
    linear_mid,
    share_mid,
    post_mid,
    post_slices,
    post_send,
    post_near,
    post_far,
    counts_mid,
    counts_own,
    far_counts,
    send_sem,
    recv_sem,
    load_sem,
):
    leaf = lax.axis_index("leaf")
    part = lax.axis_index("batch")
    devices = leaves * parts
    me = leaf * parts + part
    low_count = pixels_low.shape[0]
    mid_count = pixels_mid.shape[0]
    images = pixels_low.shape[1]
    states = trans_low.shape[2]
    share_rows = states // parts
    rows = states // devices
    wide = images * parts // HALVES

    loads = [
        pltpu.make_async_copy(source, target, load_sem.at[i])
        for i, (source, target) in enumerate(
            (
                (pixels_low_hbm, pixels_low),
                (pixels_mid_hbm, pixels_mid),
                (pixels_top_hbm, pixels_top),
                (emit_top_hbm, emit_top),
                (outside_top_hbm, outside_top),
                (emit_low_hbm, emit_low),
                (trans_low_hbm, trans_low),
                (emit_mid_hbm.at[part], emit_mid),
                (trans_mid_hbm.at[part], trans_mid),
            )
        )
    ]
    for load in loads:
        load.start()

    def slice_of(l, q):
        return pl.ds(pl.multiple_of(q * share_rows + l * rows, rows), rows)

    def quarter_of(q):
        return pl.ds(pl.multiple_of(q * share_rows, share_rows), share_rows)

    def lanes(h):
        return pl.ds(h * wide, wide)

    def send(src, dst, phase, l, q):
        pltpu.make_async_remote_copy(
            src_ref=src,
            dst_ref=dst,
            send_sem=send_sem.at[phase],
            recv_sem=recv_sem.at[phase],
            device_id=(l, q),
            device_id_type=MESH,
        ).start()

    def wait_recv(ref, phase):
        pltpu.make_async_copy(ref, ref, recv_sem.at[phase]).wait()

    def wait_send(ref, phase):
        pltpu.make_async_copy(ref, ref, send_sem.at[phase]).wait()

    def each_other(step):
        def one(k, carry):
            t = lax.rem(me + STRIDE * k, devices)
            step(t, lax.div(t, parts), lax.rem(t, parts))
            return carry

        lax.fori_loop(1, devices, one, 0)

    def each_leaf(step):
        def one(k, carry):
            step(lax.rem(leaf + 3 * k, leaves))
            return carry

        lax.fori_loop(1, leaves, one, 0)

    def each_part(step):
        def one(k, carry):
            step(lax.rem(part + k, parts))
            return carry

        lax.fori_loop(1, parts, one, 0)

    barrier = pltpu.get_barrier_semaphore()

    def greet(t, l, q):
        pl.semaphore_signal(barrier, inc=1, device_id=(l, q), device_id_type=MESH)

    each_other(greet)

    def far_row(l, carry):
        found = jnp.int32(0)
        parents = [jnp.int32(-1)] * REMOTE
        for c in range(low_count):
            parent = parent_low[l * low_count + c]
            away = lax.div(parent, mid_count) != l
            for s in range(REMOTE):
                parents[s] = jnp.where(away & (found == s), parent, parents[s])
            found = found + jnp.where(away, 1, 0)
        for s in range(REMOTE):
            far_parent[l * REMOTE + s] = parents[s]
        return carry

    lax.fori_loop(0, leaves, far_row, 0)
    found = jnp.int32(0)
    nodes = [jnp.int32(0)] * REMOTE
    for c in range(low_count):
        parent = parent_low[leaf * low_count + c]
        away = lax.div(parent, mid_count) != leaf
        for s in range(REMOTE):
            nodes[s] = jnp.where(away & (found == s), c, nodes[s])
        place[c] = jnp.where(
            away, mid_count + jnp.minimum(found, REMOTE - 1), lax.rem(parent, mid_count)
        )
        found = found + jnp.where(away, 1, 0)
    for s in range(REMOTE):
        far_index[s] = nodes[s]

    levels = lax.broadcasted_iota(jnp.int32, (emit_low.shape[1], images), 0)

    def picks(row):
        return jnp.where(levels == row, 1.0, 0.0).astype(jnp.bfloat16)

    loads[0].wait()
    loads[1].wait()
    pix[part, 0:low_count, :] = pixels_low[...]
    pix[part, low_count : low_count + mid_count, :] = pixels_mid[...]
    pl.semaphore_wait(barrier, devices - 1)
    each_part(lambda q: send(pix.at[part], pix.at[part], 0, leaf, q))
    for load in loads[2:5]:
        load.wait()
    own_top[...] = dot(emit_top[0], picks(pixels_top[...]), 0, 0) + outside_top[0].T
    mine = pl.ds(pl.multiple_of(part * images, images), images)
    each_other(
        lambda t, l, q: send(
            own_top.at[slice_of(l, q)], edge_top.at[leaf, :, mine], 1, l, q
        )
    )
    edge_top[leaf, :, mine] = own_top[slice_of(leaf, part), :]
    loads[5].wait()
    loads[6].wait()
    wait_recv(pix.at[pl.ds(0, parts - 1)], 0)

    def lookup(table, node, first, last):
        chosen = jnp.concatenate(
            [picks(pix[q, pl.ds(node, 1), :]) for q in range(first, last)], axis=1
        )
        return dot(table, chosen, 0, 0)

    def scale(inside):
        return jnp.exp(inside - jnp.max(inside, axis=0, keepdims=True))

    per = parts // HALVES
    for h in range(HALVES):

        def far(s, carry):
            node = far_index[s]
            scaled = scale(lookup(emit_low[node], node, h * per, h * per + per))
            far_up[h, s] = jnp.log(dot(trans_low[node], scaled.astype(jnp.bfloat16), 1, 0))
            return carry

        lax.fori_loop(0, REMOTE, far, 0)
        each_leaf(
            lambda l: send(
                far_up.at[h, :, slice_of(l, part), :],
                far_slices.at[h, leaf],
                10 + h,
                l,
                part,
            )
        )
        far_slices[h, leaf] = far_up[h, :, slice_of(leaf, part), :]

    loads[7].wait()
    loads[8].wait()
    inside_own[...] = lookup(emit_mid[...], low_count + part, 0, parts)

    def near(c, carry):
        scaled = scale(lookup(emit_low[c], c, 0, parts)).astype(jnp.bfloat16)
        scaled_low[c] = scaled
        linear = dot(trans_low[c], scaled, 1, 0)
        linear_full[...] = linear
        linear_low[c] = linear_full[quarter_of(part), :]
        weight = jnp.where(parent_low[leaf * low_count + c] == me, 1.0, 0.0)
        inside_own[...] += weight * jnp.log(linear)
        return carry

    lax.fori_loop(0, low_count // 2, near, 0)

    for h in range(HALVES):
        wait_recv(far_slices.at[h, pl.ds(0, leaves - 1)], 10 + h)

        def sum_far(t):
            total = jnp.zeros((rows, wide), jnp.float32)
            for l in range(leaves):
                for s in range(REMOTE):
                    weight = jnp.where(far_parent[l * REMOTE + s] == t, 1.0, 0.0)
                    total += weight * far_slices[h, l, s]
            return total

        def send_sum(t, l, q):
            mid_send[h, t] = sum_far(t)
            send(mid_send.at[h, t], mid_sums.at[h, slice_of(leaf, part)], 12 + h, l, q)

        each_other(send_sum)
        mid_sums[h, slice_of(leaf, part), :] = sum_far(me)

    lax.fori_loop(low_count // 2, low_count, near, 0)

    for h in range(HALVES):
        wait_recv(mid_sums.at[h, pl.ds(0, states - rows)], 12 + h)
        exact = scale(inside_own[:, lanes(h)] + mid_sums[h])
        post_mid[h] = exact
        scaled = exact.astype(jnp.bfloat16)
        scaled_mid[:, lanes(h)] = scaled
        linear = dot(trans_mid[...], scaled, 1, 0)
        linear_mid[h] = linear
        up_mid[h] = jnp.log(linear)
        each_other(
            lambda t, l, q: send(
                up_mid.at[h, slice_of(l, q)], up_slices.at[h, me], 14 + h, l, q
            )
        )
        up_slices[h, me] = up_mid[h, slice_of(leaf, part), :]

    wait_recv(own_top.at[pl.ds(0, states - rows)], 1)
    for h in range(HALVES):
        wait_recv(up_slices.at[h, pl.ds(0, devices - 1)], 14 + h)

        def top(r, carry):
            total = edge_top[r, :, lanes(h)]
            for p in range(devices):
                weight = jnp.where(parent_mid[p] == r, 1.0, 0.0)
                total += weight * up_slices[h, p]
            totals[h, r] = total
            return carry

        lax.fori_loop(0, leaves, top, 0)

        def send_total(t, l, q):
            total_send[h, t] = totals[h, parent_mid[t]]
            send(total_send.at[h, t], total_mine.at[h, slice_of(leaf, part)], 16 + h, l, q)

        each_other(send_total)
        total_mine[h, slice_of(leaf, part), :] = totals[h, parent_mid[me]]

    for h in range(HALVES):
        wait_recv(total_mine.at[h, pl.ds(0, states - rows)], 16 + h)
        reached = scale(total_mine[h])
        share = (
            reached / (linear_mid[h] * jnp.sum(reached, axis=0, keepdims=True))
        ).astype(jnp.bfloat16)
        share_mid[:, lanes(h)] = share
        posterior = post_mid[h] * dot(trans_mid[...], share, 0, 0)
        post_mid[h] = posterior / jnp.sum(posterior, axis=0, keepdims=True)
        each_other(
            lambda t, l, q: send(
                post_mid.at[h, slice_of(l, q)], post_slices[h].at[me], 18 + h, l, q
            )
        )
        post_slices[h][me] = post_mid[h, slice_of(leaf, part), :]
        each_part(
            lambda q: send(
                post_mid.at[h, quarter_of(q)], post_near.at[part, :, lanes(h)], 20 + h, leaf, q
            )
        )
        post_near[part, :, lanes(h)] = post_mid[h, quarter_of(part), :]

    def finished(share, scaled, weight):
        counts = dot(share, scaled, 1, 1) * weight.astype(jnp.float32) + PSEUDO
        return states * counts / jnp.sum(counts, axis=-1, keepdims=True)

    counts_own[...] = finished(share_mid[...], scaled_mid[...], trans_mid[...])
    each_part(lambda q: send(counts_own.at[quarter_of(q)], counts_mid.at[part], 2, leaf, q))
    counts_mid[part] = counts_own[quarter_of(part), :]

    landing = pl.ds(pl.multiple_of(leaf * rows, rows), rows)
    for h in range(HALVES):
        wait_recv(post_slices[h].at[pl.ds(0, devices - 1)], 18 + h)

        def pick(l):
            for s in range(REMOTE):
                parent = jnp.maximum(far_parent[l * REMOTE + s], 0)
                post_send[h, l, s] = post_slices[h][parent]

        def send_pick(l):
            pick(l)
            send(
                post_send.at[h, l],
                post_far.at[:, landing, lanes(h)],
                22 + h,
                l,
                part,
            )

        each_leaf(send_pick)
        pick(leaf)
        post_far[:, landing, lanes(h)] = post_send[h, leaf]

    def update_of(c, found):
        share = (found / linear_low[c]).astype(jnp.bfloat16)
        return finished(share, scaled_low[c], trans_low[c, quarter_of(part), :])

    for h in range(HALVES):
        wait_recv(post_mid.at[h, pl.ds(0, states - share_rows)], 20 + h)

    def near_update(c, carry):
        update_low[c] = update_of(c, post_near[jnp.minimum(place[c], mid_count - 1)])
        return carry

    lax.fori_loop(0, low_count, near_update, 0)
    wait_recv(counts_mid.at[pl.ds(0, parts - 1)], 2)
    update_mid[...] = counts_mid[...]
    for h in range(HALVES):
        wait_recv(post_send.at[h, pl.ds(0, leaves - 1)], 22 + h)

    def far_update(s, carry):
        far_counts[s] = update_of(far_index[s], post_far[s])
        return carry

    lax.fori_loop(0, REMOTE, far_update, 0)

    def choose(c, carry):
        slot = place[c] - mid_count
        update_low[c] = jnp.where(
            slot >= 0, far_counts[jnp.maximum(slot, 0)], update_low[c]
        )
        return carry

    lax.fori_loop(0, low_count, choose, 0)

    wait_send(pix.at[pl.ds(0, parts - 1)], 0)
    wait_send(own_top.at[pl.ds(0, states - rows)], 1)
    wait_send(counts_mid.at[pl.ds(0, parts - 1)], 2)
    for h in range(HALVES):
        wait_send(far_slices.at[h, pl.ds(0, leaves - 1)], 10 + h)
        wait_send(mid_send.at[h, pl.ds(0, devices - 1)], 12 + h)
        wait_send(up_slices.at[h, pl.ds(0, devices - 1)], 14 + h)
        wait_send(total_send.at[h, pl.ds(0, devices - 1)], 16 + h)
        wait_send(post_slices[h].at[pl.ds(0, devices - 1)], 18 + h)
        wait_send(post_mid.at[h, pl.ds(0, states - share_rows)], 20 + h)
        wait_send(post_send.at[h, pl.ds(0, leaves - 1)], 22 + h)


def fused(
    leaves,
    parts,
    pixels_low,
    pixels_mid,
    pixels_top,
    emit_low,
    emit_mid,
    emit_top,
    trans_low,
    trans_mid,
    outside_top,
    parent_low,
    parent_mid,
):
    low_count, images = pixels_low.shape
    mid_count = pixels_mid.shape[0]
    states = trans_low.shape[2]
    devices = leaves * parts
    share_rows = states // parts
    rows = states // devices
    whole = images * parts
    wide = whole // HALVES
    held = -(-(low_count + mid_count) // 8) * 8
    real, half = jnp.float32, jnp.bfloat16
    vmem = pltpu.VMEM
    arrays = (pixels_low, pixels_mid, pixels_top, emit_low, emit_mid, emit_top, trans_low)
    arrays += (trans_mid, outside_top)
    return pl.pallas_call(
        functools.partial(kernel, leaves, parts),
        out_shape=(
            jax.ShapeDtypeStruct((low_count, share_rows, states), real),
            jax.ShapeDtypeStruct((mid_count, share_rows, states), real),
        ),
        in_specs=[pl.BlockSpec(memory_space=pltpu.SMEM)] * 2
        + [pl.BlockSpec(memory_space=pltpu.HBM)] * len(arrays),
        out_specs=(pl.BlockSpec(memory_space=pltpu.VMEM),) * 2,
        scratch_shapes=[
            pltpu.SMEM((REMOTE,), jnp.int32),
            pltpu.SMEM((leaves * REMOTE,), jnp.int32),
            pltpu.SMEM((low_count,), jnp.int32),
            vmem(pixels_low.shape, jnp.int32),
            vmem(pixels_mid.shape, jnp.int32),
            vmem(pixels_top.shape, jnp.int32),
            vmem(emit_low.shape, half),
            vmem(emit_mid.shape[1:], half),
            vmem(emit_top.shape, half),
            vmem(trans_low.shape, half),
            vmem(trans_mid.shape[1:], half),
            vmem(outside_top.shape, real),
            vmem((parts, held, images), jnp.int32),
            vmem((leaves, rows, whole), real),
            vmem((states, images), real),
            vmem((HALVES, REMOTE, states, wide), real),
            vmem((HALVES, leaves, REMOTE, rows, wide), real),
            vmem((HALVES, devices, rows, wide), real),
            vmem((HALVES, states, wide), real),
            vmem((states, whole), real),
            vmem((low_count, states, whole), half),
            vmem((low_count, share_rows, whole), real),
            vmem((states, whole), real),
            vmem((HALVES, states, wide), real),
            vmem((HALVES, devices, rows, wide), real),
            vmem((HALVES, leaves, rows, wide), real),
            vmem((HALVES, devices, rows, wide), real),
            vmem((HALVES, states, wide), real),
            vmem((states, whole), half),
            vmem((HALVES, states, wide), real),
            vmem((states, whole), half),
            vmem((HALVES, states, wide), real),
            (vmem((devices, rows, wide), real),) * HALVES,
            vmem((HALVES, leaves, REMOTE, rows, wide), real),
            vmem((mid_count, share_rows, whole), real),
            vmem((REMOTE, share_rows, whole), real),
            vmem((mid_count, share_rows, states), real),
            vmem((states, states), real),
            vmem((REMOTE, share_rows, states), real),
            pltpu.SemaphoreType.DMA((24,)),
            pltpu.SemaphoreType.DMA((24,)),
            pltpu.SemaphoreType.DMA((len(arrays),)),
        ],
        compiler_params=pltpu.CompilerParams(
            collective_id=0, has_side_effects=True, vmem_limit_bytes=62 * 2**20
        ),
    )(parent_low, parent_mid, *arrays)


def solution(mesh):
    leaves, parts = mesh.shape["leaf"], mesh.shape["batch"]
    fits = 256 % (8 * leaves * parts) == 0
    chosen = functools.partial(fused, leaves, parts) if fits else body
    return jax.shard_map(
        chosen,
        mesh=mesh,
        in_specs=(
            P("leaf", "batch"),
            P("leaf", "batch"),
            P("leaf", "batch"),
            P("leaf", None, None),
            P("leaf", None, None),
            P("leaf", None, None),
            P("leaf", None, None),
            P("leaf", None, None),
            P("leaf", "batch", None),
            P(),
            P(),
        ),
        out_specs=(P("leaf", "batch", None), P("leaf", "batch", None)),
        check_vma=False,
    )
```

```python
import functools

import jax
import jax.numpy as jnp
from jax import lax
from jax.experimental import pallas as pl
from jax.experimental.pallas import tpu as pltpu
from jax.sharding import PartitionSpec as P

PSEUDO = 0.001
REMOTE = 3
HALVES = 2
STRIDE = 13
MESH = pl.DeviceIdType.MESH


def lookup_all(table, pixels):
    levels = jnp.arange(table.shape[1], dtype=jnp.int32)
    picks = (pixels[:, :, None] == levels[None, None, :]).astype(jnp.bfloat16)
    return jnp.einsum("nbv,nvk->nbk", picks, table, preferred_element_type=jnp.float32)


def upward_all(inside, weight):
    top = jnp.max(inside, axis=-1, keepdims=True)
    scaled = jnp.exp(inside - top).astype(jnp.bfloat16)
    linear = jnp.einsum("nbj,nij->nbi", scaled, weight, preferred_element_type=jnp.float32)
    return (jnp.log(linear) + top, scaled)


def edge_all(above, weight, scaled):
    peak = jnp.max(above, axis=-1, keepdims=True)
    pushed = jnp.exp(above - peak).astype(jnp.bfloat16)
    reach = jnp.einsum("nbi,nij->nbj", pushed, weight, preferred_element_type=jnp.float32)
    total = jnp.sum(reach * scaled.astype(jnp.float32), axis=-1, keepdims=True)
    share = (pushed.astype(jnp.float32) / total).astype(jnp.bfloat16)
    counts = jnp.einsum("nbi,nbj->nij", share, scaled, preferred_element_type=jnp.float32)
    return (counts * weight.astype(jnp.float32), jnp.log(reach) + peak)


def finish(summed):
    counts = summed + PSEUDO
    return counts.shape[-1] * counts / jnp.sum(counts, axis=-1, keepdims=True)


def body(
    pixels_low,
    pixels_mid,
    pixels_top,
    emit_low,
    emit_mid,
    emit_top,
    trans_low,
    trans_mid,
    outside_top,
    parent_low,
    parent_mid,
):
    devices = lax.axis_size("leaf")
    mid_count = emit_mid.shape[0]
    top_count = emit_top.shape[0]
    up_low, scaled_low = upward_all(lookup_all(emit_low, pixels_low), trans_low)
    emis_mid = lookup_all(emit_mid, pixels_mid)
    emis_top = lookup_all(emit_top, pixels_top)
    moved = lax.all_to_all(up_low, "leaf", split_axis=1, concat_axis=0, tiled=True)
    gathered_mid = jax.ops.segment_sum(moved, parent_low, num_segments=mid_count * devices)
    sums_mid = lax.all_to_all(gathered_mid, "leaf", split_axis=0, concat_axis=1, tiled=True)
    inside_mid = emis_mid + sums_mid
    up_mid, scaled_mid = upward_all(inside_mid, trans_mid)
    moved_mid = lax.all_to_all(up_mid, "leaf", split_axis=1, concat_axis=0, tiled=True)
    gathered_top = jax.ops.segment_sum(moved_mid, parent_mid, num_segments=top_count * devices)
    sums_top = lax.all_to_all(gathered_top, "leaf", split_axis=0, concat_axis=1, tiled=True)
    total_top = emis_top + sums_top + outside_top
    spread_top = lax.all_to_all(total_top, "leaf", split_axis=1, concat_axis=0, tiled=True)
    picked = lax.all_to_all(spread_top[parent_mid], "leaf", split_axis=0, concat_axis=1, tiled=True)
    counts_mid, outside_mid = edge_all(picked - up_mid, trans_mid, scaled_mid)
    update_mid = finish(lax.psum_scatter(counts_mid, "batch", scatter_dimension=1, tiled=True))
    total_mid = inside_mid + outside_mid
    spread_mid = lax.all_to_all(total_mid, "leaf", split_axis=1, concat_axis=0, tiled=True)
    above_low = lax.all_to_all(
        spread_mid[parent_low], "leaf", split_axis=0, concat_axis=1, tiled=True
    )
    counts_low, unused = edge_all(above_low - up_low, trans_low, scaled_low)
    update_low = finish(lax.psum_scatter(counts_low, "batch", scatter_dimension=1, tiled=True))
    return (update_low, update_mid)


def dot(a, b, left, right):
    return lax.dot_general(
        a, b, (((left,), (right,)), ((), ())), preferred_element_type=jnp.float32
    )


def kernel(
    leaves,
    parts,
    parent_low,
    parent_mid,
    pixels_low_hbm,
    pixels_mid_hbm,
    pixels_top_hbm,
    emit_low_hbm,
    emit_mid_hbm,
    emit_top_hbm,
    trans_low_hbm,
    trans_mid_hbm,
    outside_top_hbm,
    update_low,
    update_mid,
    far_index,
    far_parent,
    place,
    pixels_low,
    pixels_mid,
    pixels_top,
    emit_low,
    emit_mid,
    emit_top,
    trans_low,
    trans_mid,
    outside_top,
    pix,
    edge_top,
    own_top,
    far_up,
    far_slices,
    mid_send,
    mid_sums,
    inside_own,
    scaled_low,
    linear_low,
    linear_full,
    up_mid,
    up_slices,
    partial_own,
    partial_far,
    totals,
    total_send,
    total_mine,
    scaled_mid,
    linear_mid,
    share_mid,
    post_mid,
    post_slices,
    post_send,
    post_near,
    post_far,
    counts_mid,
    counts_own,
    far_counts,
    send_sem,
    recv_sem,
    load_sem,
):
    leaf = lax.axis_index("leaf")
    part = lax.axis_index("batch")
    devices = leaves * parts
    me = leaf * parts + part
    low_count = pixels_low.shape[0]
    mid_count = pixels_mid.shape[0]
    images = pixels_low.shape[1]
    states = trans_low.shape[2]
    share_rows = states // parts
    rows = states // devices
    wide = images * parts // HALVES

    loads = [
        pltpu.make_async_copy(source, target, load_sem.at[i])
        for i, (source, target) in enumerate(
            (
                (pixels_low_hbm, pixels_low),
                (emit_low_hbm, emit_low),
                (trans_low_hbm, trans_low),
                (pixels_mid_hbm, pixels_mid),
                (pixels_top_hbm, pixels_top),
                (emit_top_hbm, emit_top),
                (outside_top_hbm, outside_top),
                (emit_mid_hbm.at[part], emit_mid),
                (trans_mid_hbm.at[part], trans_mid),
            )
        )
    ]
    for load in loads:
        load.start()

    def slice_of(l, q):
        return pl.ds(pl.multiple_of(q * share_rows + l * rows, rows), rows)

    def quarter_of(q):
        return pl.ds(pl.multiple_of(q * share_rows, share_rows), share_rows)

    side = leaves // 2
    pairs = devices // 2
    base = lax.div(leaf, side) * side
    spot = lax.rem(me, pairs)

    def tall_slice_of(l, q):
        start = q * share_rows + lax.rem(l, side) * (2 * rows)
        return pl.ds(pl.multiple_of(start, 2 * rows), 2 * rows)

    def each_near(step):
        def one(k, carry):
            t = lax.rem(spot + 5 * k, pairs)
            step(t, base + lax.div(t, parts), lax.rem(t, parts))
            return carry

        lax.fori_loop(1, pairs, one, 0)

    def lanes(h):
        return pl.ds(h * wide, wide)

    def send(src, dst, phase, l, q):
        pltpu.make_async_remote_copy(
            src_ref=src,
            dst_ref=dst,
            send_sem=send_sem.at[phase],
            recv_sem=recv_sem.at[phase],
            device_id=(l, q),
            device_id_type=MESH,
        ).start()

    def wait_recv(ref, phase):
        pltpu.make_async_copy(ref, ref, recv_sem.at[phase]).wait()

    def wait_send(ref, phase):
        pltpu.make_async_copy(ref, ref, send_sem.at[phase]).wait()

    def each_other(step):
        def one(k, carry):
            t = lax.rem(me + STRIDE * k, devices)
            step(t, lax.div(t, parts), lax.rem(t, parts))
            return carry

        lax.fori_loop(1, devices, one, 0)

    def each_leaf(step):
        def one(k, carry):
            step(lax.rem(leaf + 3 * k, leaves))
            return carry

        lax.fori_loop(1, leaves, one, 0)

    def each_part(step):
        def one(k, carry):
            step(lax.rem(part + k, parts))
            return carry

        lax.fori_loop(1, parts, one, 0)

    barrier = pltpu.get_barrier_semaphore()

    def greet(t, l, q):
        pl.semaphore_signal(barrier, inc=1, device_id=(l, q), device_id_type=MESH)

    each_other(greet)

    def far_row(l, carry):
        found = jnp.int32(0)
        parents = [jnp.int32(-1)] * REMOTE
        for c in range(low_count):
            parent = parent_low[l * low_count + c]
            away = lax.div(parent, mid_count) != l
            for s in range(REMOTE):
                parents[s] = jnp.where(away & (found == s), parent, parents[s])
            found = found + jnp.where(away, 1, 0)
        for s in range(REMOTE):
            far_parent[l * REMOTE + s] = parents[s]
        return carry

    lax.fori_loop(0, leaves, far_row, 0)
    found = jnp.int32(0)
    nodes = [jnp.int32(0)] * REMOTE
    for c in range(low_count):
        parent = parent_low[leaf * low_count + c]
        away = lax.div(parent, mid_count) != leaf
        for s in range(REMOTE):
            nodes[s] = jnp.where(away & (found == s), c, nodes[s])
        place[c] = jnp.where(
            away, mid_count + jnp.minimum(found, REMOTE - 1), lax.rem(parent, mid_count)
        )
        found = found + jnp.where(away, 1, 0)
    for s in range(REMOTE):
        far_index[s] = nodes[s]

    levels = lax.broadcasted_iota(jnp.int32, (emit_low.shape[1], images), 0)

    def picks(row):
        return jnp.where(levels == row, 1.0, 0.0).astype(jnp.bfloat16)

    def scale(inside):
        return jnp.exp(inside - jnp.max(inside, axis=0, keepdims=True))

    for load in loads[0:3]:
        load.wait()

    def far(s, carry):
        node = far_index[s]
        inside = dot(emit_low[node], picks(pixels_low[pl.ds(node, 1), :]), 0, 0)
        scaled = scale(inside).astype(jnp.bfloat16)
        far_up[s] = jnp.log(dot(trans_low[node], scaled, 1, 0))
        return carry

    lax.fori_loop(0, REMOTE, far, 0)
    mine = pl.ds(pl.multiple_of(part * images, images), images)
    loads[3].wait()
    pix[part, 0:low_count, :] = pixels_low[...]
    pix[part, low_count : low_count + mid_count, :] = pixels_mid[...]
    pl.semaphore_wait(barrier, devices - 1)
    each_part(lambda q: send(pix.at[part], pix.at[part], 0, leaf, q))
    each_other(
        lambda t, l, q: send(
            far_up.at[:, slice_of(l, q), :], far_slices.at[leaf, :, :, mine], 3, l, q
        )
    )
    far_slices[leaf, :, :, mine] = far_up[:, slice_of(leaf, part), :]
    for load in loads[4:7]:
        load.wait()
    own_top[...] = dot(emit_top[0], picks(pixels_top[...]), 0, 0) + outside_top[0].T
    each_near(
        lambda t, l, q: send(
            own_top.at[tall_slice_of(l, q)],
            edge_top.at[lax.rem(leaf, side), :, mine],
            1,
            l,
            q,
        )
    )
    edge_top[lax.rem(leaf, side), :, mine] = own_top[tall_slice_of(leaf, part), :]
    wait_recv(pix.at[pl.ds(0, parts - 1)], 0)

    def lookup(table, node):
        chosen = jnp.concatenate(
            [picks(pix[q, pl.ds(node, 1), :]) for q in range(parts)], axis=1
        )
        return dot(table, chosen, 0, 0)

    loads[7].wait()
    loads[8].wait()
    inside_own[...] = lookup(emit_mid[...], low_count + part)

    def near(c, carry):
        scaled = scale(lookup(emit_low[c], c)).astype(jnp.bfloat16)
        scaled_low[c] = scaled
        linear = dot(trans_low[c], scaled, 1, 0)
        linear_full[...] = linear
        linear_low[c] = linear_full[quarter_of(part), :]
        weight = jnp.where(parent_low[leaf * low_count + c] == me, 1.0, 0.0)
        inside_own[...] += weight * jnp.log(linear)
        return carry

    lax.fori_loop(0, low_count // 2, near, 0)

    wait_recv(far_up.at[:, pl.ds(0, states - rows)], 3)
    for h in range(HALVES):

        def sum_far(t):
            total = jnp.zeros((rows, wide), jnp.float32)
            for l in range(leaves):
                for s in range(REMOTE):
                    weight = jnp.where(far_parent[l * REMOTE + s] == t, 1.0, 0.0)
                    total += weight * far_slices[l, s, :, lanes(h)]
            return total

        def send_sum(t, l, q):
            mid_send[h, t] = sum_far(t)
            send(mid_send.at[h, t], mid_sums.at[h, slice_of(leaf, part)], 12 + h, l, q)

        each_other(send_sum)
        mid_sums[h, slice_of(leaf, part), :] = sum_far(me)

    lax.fori_loop(low_count // 2, low_count, near, 0)

    for h in range(HALVES):
        wait_recv(mid_sums.at[h, pl.ds(0, states - rows)], 12 + h)
        exact = scale(inside_own[:, lanes(h)] + mid_sums[h])
        post_mid[h] = exact
        scaled = exact.astype(jnp.bfloat16)
        scaled_mid[:, lanes(h)] = scaled
        linear = dot(trans_mid[...], scaled, 1, 0)
        linear_mid[h] = linear
        up_mid[h] = jnp.log(linear)
        each_near(
            lambda t, l, q: send(
                up_mid.at[h, tall_slice_of(l, q)], up_slices.at[h, spot], 14 + h, l, q
            )
        )
        up_slices[h, spot] = up_mid[h, tall_slice_of(leaf, part), :]

    wait_recv(own_top.at[pl.ds(0, states - 2 * rows)], 1)
    for h in range(HALVES):
        wait_recv(up_slices.at[h, pl.ds(0, pairs - 1)], 14 + h)

        def top(r, carry):
            here = jnp.where(lax.div(r, side) == lax.div(leaf, side), 1.0, 0.0)
            total = here * edge_top[lax.rem(r, side), :, lanes(h)]
            for p in range(pairs):
                weight = jnp.where(parent_mid[base * parts + p] == r, 1.0, 0.0)
                total += weight * up_slices[h, p]
            partial_own[h, r] = total
            return carry

        lax.fori_loop(0, leaves, top, 0)
        send(partial_own.at[h], partial_far.at[h], 24 + h, lax.rem(leaf + side, leaves), part)

    for h in range(HALVES):
        wait_recv(partial_far.at[h], 24 + h)
        totals[h] = partial_own[h] + partial_far[h]

        def send_total(t, l, q):
            total_send[h, t] = totals[h, parent_mid[base * parts + t]]
            send(
                total_send.at[h, t], total_mine.at[h, tall_slice_of(leaf, part)], 16 + h, l, q
            )

        each_near(send_total)
        total_mine[h, tall_slice_of(leaf, part), :] = totals[h, parent_mid[me]]

    for h in range(HALVES):
        wait_recv(total_mine.at[h, pl.ds(0, states - 2 * rows)], 16 + h)
        reached = scale(total_mine[h])
        share = (
            reached / (linear_mid[h] * jnp.sum(reached, axis=0, keepdims=True))
        ).astype(jnp.bfloat16)
        share_mid[:, lanes(h)] = share
        posterior = post_mid[h] * dot(trans_mid[...], share, 0, 0)
        post_mid[h] = posterior / jnp.sum(posterior, axis=0, keepdims=True)
        each_other(
            lambda t, l, q: send(
                post_mid.at[h, slice_of(l, q)], post_slices[h].at[me], 18 + h, l, q
            )
        )
        post_slices[h][me] = post_mid[h, slice_of(leaf, part), :]
        each_part(
            lambda q: send(
                post_mid.at[h, quarter_of(q)], post_near.at[part, :, lanes(h)], 20 + h, leaf, q
            )
        )
        post_near[part, :, lanes(h)] = post_mid[h, quarter_of(part), :]

    def finished(share, scaled, weight):
        counts = dot(share, scaled, 1, 1) * weight.astype(jnp.float32) + PSEUDO
        return states * counts / jnp.sum(counts, axis=-1, keepdims=True)

    counts_own[...] = finished(share_mid[...], scaled_mid[...], trans_mid[...])
    each_part(lambda q: send(counts_own.at[quarter_of(q)], counts_mid.at[part], 2, leaf, q))
    counts_mid[part] = counts_own[quarter_of(part), :]

    landing = pl.ds(pl.multiple_of(leaf * rows, rows), rows)
    for h in range(HALVES):
        wait_recv(post_slices[h].at[pl.ds(0, devices - 1)], 18 + h)

        def pick(l):
            for s in range(REMOTE):
                parent = jnp.maximum(far_parent[l * REMOTE + s], 0)
                post_send[h, l, s] = post_slices[h][parent]

        def send_pick(l):
            pick(l)
            send(
                post_send.at[h, l],
                post_far.at[:, landing, lanes(h)],
                22 + h,
                l,
                part,
            )

        each_leaf(send_pick)
        pick(leaf)
        post_far[:, landing, lanes(h)] = post_send[h, leaf]

    def update_of(c, found):
        share = (found / linear_low[c]).astype(jnp.bfloat16)
        return finished(share, scaled_low[c], trans_low[c, quarter_of(part), :])

    for h in range(HALVES):
        wait_recv(post_mid.at[h, pl.ds(0, states - share_rows)], 20 + h)

    def near_update(c, carry):
        update_low[c] = update_of(c, post_near[jnp.minimum(place[c], mid_count - 1)])
        return carry

    lax.fori_loop(0, low_count, near_update, 0)
    wait_recv(counts_mid.at[pl.ds(0, parts - 1)], 2)
    update_mid[...] = counts_mid[...]
    for h in range(HALVES):
        wait_recv(post_send.at[h, pl.ds(0, leaves - 1)], 22 + h)

    def far_update(s, carry):
        far_counts[s] = update_of(far_index[s], post_far[s])
        return carry

    lax.fori_loop(0, REMOTE, far_update, 0)

    def choose(c, carry):
        slot = place[c] - mid_count
        update_low[c] = jnp.where(
            slot >= 0, far_counts[jnp.maximum(slot, 0)], update_low[c]
        )
        return carry

    lax.fori_loop(0, low_count, choose, 0)

    wait_send(pix.at[pl.ds(0, parts - 1)], 0)
    wait_send(own_top.at[pl.ds(0, states - 2 * rows)], 1)
    wait_send(counts_mid.at[pl.ds(0, parts - 1)], 2)
    wait_send(far_up.at[:, pl.ds(0, states - rows)], 3)
    for h in range(HALVES):
        wait_send(mid_send.at[h, pl.ds(0, devices - 1)], 12 + h)
        wait_send(up_slices.at[h, pl.ds(0, pairs - 1)], 14 + h)
        wait_send(total_send.at[h, pl.ds(0, pairs - 1)], 16 + h)
        wait_send(partial_own.at[h], 24 + h)
        wait_send(post_slices[h].at[pl.ds(0, devices - 1)], 18 + h)
        wait_send(post_mid.at[h, pl.ds(0, states - share_rows)], 20 + h)
        wait_send(post_send.at[h, pl.ds(0, leaves - 1)], 22 + h)


def fused(
    leaves,
    parts,
    pixels_low,
    pixels_mid,
    pixels_top,
    emit_low,
    emit_mid,
    emit_top,
    trans_low,
    trans_mid,
    outside_top,
    parent_low,
    parent_mid,
):
    low_count, images = pixels_low.shape
    mid_count = pixels_mid.shape[0]
    states = trans_low.shape[2]
    devices = leaves * parts
    share_rows = states // parts
    rows = states // devices
    whole = images * parts
    wide = whole // HALVES
    held = -(-(low_count + mid_count) // 8) * 8
    real, half = jnp.float32, jnp.bfloat16
    vmem = pltpu.VMEM
    arrays = (pixels_low, pixels_mid, pixels_top, emit_low, emit_mid, emit_top, trans_low)
    arrays += (trans_mid, outside_top)
    return pl.pallas_call(
        functools.partial(kernel, leaves, parts),
        out_shape=(
            jax.ShapeDtypeStruct((low_count, share_rows, states), real),
            jax.ShapeDtypeStruct((mid_count, share_rows, states), real),
        ),
        in_specs=[pl.BlockSpec(memory_space=pltpu.SMEM)] * 2
        + [pl.BlockSpec(memory_space=pltpu.HBM)] * len(arrays),
        out_specs=(pl.BlockSpec(memory_space=pltpu.VMEM),) * 2,
        scratch_shapes=[
            pltpu.SMEM((REMOTE,), jnp.int32),
            pltpu.SMEM((leaves * REMOTE,), jnp.int32),
            pltpu.SMEM((low_count,), jnp.int32),
            vmem(pixels_low.shape, jnp.int32),
            vmem(pixels_mid.shape, jnp.int32),
            vmem(pixels_top.shape, jnp.int32),
            vmem(emit_low.shape, half),
            vmem(emit_mid.shape[1:], half),
            vmem(emit_top.shape, half),
            vmem(trans_low.shape, half),
            vmem(trans_mid.shape[1:], half),
            vmem(outside_top.shape, real),
            vmem((parts, held, images), jnp.int32),
            vmem((leaves // 2, 2 * rows, whole), real),
            vmem((states, images), real),
            vmem((REMOTE, states, images), real),
            vmem((leaves, REMOTE, rows, whole), real),
            vmem((HALVES, devices, rows, wide), real),
            vmem((HALVES, states, wide), real),
            vmem((states, whole), real),
            vmem((low_count, states, whole), half),
            vmem((low_count, share_rows, whole), real),
            vmem((states, whole), real),
            vmem((HALVES, states, wide), real),
            vmem((HALVES, devices // 2, 2 * rows, wide), real),
            vmem((HALVES, leaves, 2 * rows, wide), real),
            vmem((HALVES, leaves, 2 * rows, wide), real),
            vmem((HALVES, leaves, 2 * rows, wide), real),
            vmem((HALVES, devices // 2, 2 * rows, wide), real),
            vmem((HALVES, states, wide), real),
            vmem((states, whole), half),
            vmem((HALVES, states, wide), real),
            vmem((states, whole), half),
            vmem((HALVES, states, wide), real),
            (vmem((devices, rows, wide), real),) * HALVES,
            vmem((HALVES, leaves, REMOTE, rows, wide), real),
            vmem((mid_count, share_rows, whole), real),
            vmem((REMOTE, share_rows, whole), real),
            vmem((mid_count, share_rows, states), real),
            vmem((states, states), real),
            vmem((REMOTE, share_rows, states), real),
            pltpu.SemaphoreType.DMA((26,)),
            pltpu.SemaphoreType.DMA((26,)),
            pltpu.SemaphoreType.DMA((len(arrays),)),
        ],
        compiler_params=pltpu.CompilerParams(
            collective_id=0, has_side_effects=True, vmem_limit_bytes=62 * 2**20
        ),
    )(parent_low, parent_mid, *arrays)


def solution(mesh):
    leaves, parts = mesh.shape["leaf"], mesh.shape["batch"]
    fits = leaves % 2 == 0 and 256 % (8 * leaves * parts) == 0
    chosen = functools.partial(fused, leaves, parts) if fits else body
    return jax.shard_map(
        chosen,
        mesh=mesh,
        in_specs=(
            P("leaf", "batch"),
            P("leaf", "batch"),
            P("leaf", "batch"),
            P("leaf", None, None),
            P("leaf", None, None),
            P("leaf", None, None),
            P("leaf", None, None),
            P("leaf", None, None),
            P("leaf", "batch", None),
            P(),
            P(),
        ),
        out_specs=(P("leaf", "batch", None), P("leaf", "batch", None)),
        check_vma=False,
    )
```

```python
import functools

import jax
import jax.numpy as jnp
from jax import lax
from jax.experimental import pallas as pl
from jax.experimental.pallas import tpu as pltpu
from jax.sharding import PartitionSpec as P

PSEUDO = 0.001
REMOTE = 3
HALVES = 2
STRIDE = 13
MESH = pl.DeviceIdType.MESH


def lookup_all(table, pixels):
    levels = jnp.arange(table.shape[1], dtype=jnp.int32)
    picks = (pixels[:, :, None] == levels[None, None, :]).astype(jnp.bfloat16)
    return jnp.einsum("nbv,nvk->nbk", picks, table, preferred_element_type=jnp.float32)


def upward_all(inside, weight):
    top = jnp.max(inside, axis=-1, keepdims=True)
    scaled = jnp.exp(inside - top).astype(jnp.bfloat16)
    linear = jnp.einsum("nbj,nij->nbi", scaled, weight, preferred_element_type=jnp.float32)
    return (jnp.log(linear) + top, scaled)


def edge_all(above, weight, scaled):
    peak = jnp.max(above, axis=-1, keepdims=True)
    pushed = jnp.exp(above - peak).astype(jnp.bfloat16)
    reach = jnp.einsum("nbi,nij->nbj", pushed, weight, preferred_element_type=jnp.float32)
    total = jnp.sum(reach * scaled.astype(jnp.float32), axis=-1, keepdims=True)
    share = (pushed.astype(jnp.float32) / total).astype(jnp.bfloat16)
    counts = jnp.einsum("nbi,nbj->nij", share, scaled, preferred_element_type=jnp.float32)
    return (counts * weight.astype(jnp.float32), jnp.log(reach) + peak)


def finish(summed):
    counts = summed + PSEUDO
    return counts.shape[-1] * counts / jnp.sum(counts, axis=-1, keepdims=True)


def body(
    pixels_low,
    pixels_mid,
    pixels_top,
    emit_low,
    emit_mid,
    emit_top,
    trans_low,
    trans_mid,
    outside_top,
    parent_low,
    parent_mid,
):
    devices = lax.axis_size("leaf")
    mid_count = emit_mid.shape[0]
    top_count = emit_top.shape[0]
    up_low, scaled_low = upward_all(lookup_all(emit_low, pixels_low), trans_low)
    emis_mid = lookup_all(emit_mid, pixels_mid)
    emis_top = lookup_all(emit_top, pixels_top)
    moved = lax.all_to_all(up_low, "leaf", split_axis=1, concat_axis=0, tiled=True)
    gathered_mid = jax.ops.segment_sum(moved, parent_low, num_segments=mid_count * devices)
    sums_mid = lax.all_to_all(gathered_mid, "leaf", split_axis=0, concat_axis=1, tiled=True)
    inside_mid = emis_mid + sums_mid
    up_mid, scaled_mid = upward_all(inside_mid, trans_mid)
    moved_mid = lax.all_to_all(up_mid, "leaf", split_axis=1, concat_axis=0, tiled=True)
    gathered_top = jax.ops.segment_sum(moved_mid, parent_mid, num_segments=top_count * devices)
    sums_top = lax.all_to_all(gathered_top, "leaf", split_axis=0, concat_axis=1, tiled=True)
    total_top = emis_top + sums_top + outside_top
    spread_top = lax.all_to_all(total_top, "leaf", split_axis=1, concat_axis=0, tiled=True)
    picked = lax.all_to_all(spread_top[parent_mid], "leaf", split_axis=0, concat_axis=1, tiled=True)
    counts_mid, outside_mid = edge_all(picked - up_mid, trans_mid, scaled_mid)
    update_mid = finish(lax.psum_scatter(counts_mid, "batch", scatter_dimension=1, tiled=True))
    total_mid = inside_mid + outside_mid
    spread_mid = lax.all_to_all(total_mid, "leaf", split_axis=1, concat_axis=0, tiled=True)
    above_low = lax.all_to_all(
        spread_mid[parent_low], "leaf", split_axis=0, concat_axis=1, tiled=True
    )
    counts_low, unused = edge_all(above_low - up_low, trans_low, scaled_low)
    update_low = finish(lax.psum_scatter(counts_low, "batch", scatter_dimension=1, tiled=True))
    return (update_low, update_mid)


def dot(a, b, left, right):
    return lax.dot_general(
        a, b, (((left,), (right,)), ((), ())), preferred_element_type=jnp.float32
    )


def kernel(
    leaves,
    parts,
    parent_low,
    parent_mid,
    pixels_low_hbm,
    pixels_mid_hbm,
    pixels_top_hbm,
    emit_low_hbm,
    emit_mid_hbm,
    emit_top_hbm,
    trans_low_hbm,
    trans_mid_hbm,
    outside_top_hbm,
    update_low,
    update_mid,
    far_index,
    far_parent,
    place,
    pixels_low,
    pixels_mid,
    pixels_top,
    emit_low,
    emit_mid,
    emit_top,
    trans_low,
    trans_mid,
    outside_top,
    pix,
    edge_top,
    own_top,
    far_up,
    far_slices,
    mid_send,
    mid_sums,
    inside_own,
    scaled_low,
    linear_low,
    near_sums,
    inside_near,
    up_mid,
    up_slices,
    partial_own,
    partial_far,
    totals,
    total_send,
    total_mine,
    scaled_mid,
    linear_mid,
    share_mid,
    post_mid,
    post_slices,
    post_send,
    post_near,
    post_far,
    counts_mid,
    counts_own,
    far_counts,
    send_sem,
    recv_sem,
    load_sem,
):
    leaf = lax.axis_index("leaf")
    part = lax.axis_index("batch")
    devices = leaves * parts
    me = leaf * parts + part
    low_count = pixels_low.shape[0]
    mid_count = pixels_mid.shape[0]
    images = pixels_low.shape[1]
    states = trans_low.shape[2]
    share_rows = states // parts
    rows = states // devices
    wide = images * parts // HALVES

    loads = [
        pltpu.make_async_copy(source, target, load_sem.at[i])
        for i, (source, target) in enumerate(
            (
                (pixels_low_hbm, pixels_low),
                (emit_low_hbm, emit_low),
                (trans_low_hbm, trans_low),
                (pixels_mid_hbm, pixels_mid),
                (pixels_top_hbm, pixels_top),
                (emit_top_hbm, emit_top),
                (outside_top_hbm, outside_top),
                (emit_mid_hbm.at[part], emit_mid),
                (trans_mid_hbm.at[part], trans_mid),
            )
        )
    ]
    for load in loads:
        load.start()

    def slice_of(l, q):
        return pl.ds(pl.multiple_of(q * share_rows + l * rows, rows), rows)

    def quarter_of(q):
        return pl.ds(pl.multiple_of(q * share_rows, share_rows), share_rows)

    side = leaves // 2
    pairs = devices // 2
    base = lax.div(leaf, side) * side
    spot = lax.rem(me, pairs)

    def tall_slice_of(l, q):
        start = q * share_rows + lax.rem(l, side) * (2 * rows)
        return pl.ds(pl.multiple_of(start, 2 * rows), 2 * rows)

    def each_near(step):
        def one(k, carry):
            t = lax.rem(spot + 5 * k, pairs)
            step(t, base + lax.div(t, parts), lax.rem(t, parts))
            return carry

        lax.fori_loop(1, pairs, one, 0)

    def lanes(h):
        return pl.ds(h * wide, wide)

    def send(src, dst, phase, l, q):
        pltpu.make_async_remote_copy(
            src_ref=src,
            dst_ref=dst,
            send_sem=send_sem.at[phase],
            recv_sem=recv_sem.at[phase],
            device_id=(l, q),
            device_id_type=MESH,
        ).start()

    def wait_recv(ref, phase):
        pltpu.make_async_copy(ref, ref, recv_sem.at[phase]).wait()

    def wait_send(ref, phase):
        pltpu.make_async_copy(ref, ref, send_sem.at[phase]).wait()

    def each_other(step):
        def one(k, carry):
            t = lax.rem(me + STRIDE * k, devices)
            step(t, lax.div(t, parts), lax.rem(t, parts))
            return carry

        lax.fori_loop(1, devices, one, 0)

    def each_leaf(step):
        def one(k, carry):
            step(lax.rem(leaf + 3 * k, leaves))
            return carry

        lax.fori_loop(1, leaves, one, 0)

    def each_part(step):
        def one(k, carry):
            step(lax.rem(part + k, parts))
            return carry

        lax.fori_loop(1, parts, one, 0)

    barrier = pltpu.get_barrier_semaphore()

    def greet(t, l, q):
        pl.semaphore_signal(barrier, inc=1, device_id=(l, q), device_id_type=MESH)

    each_other(greet)

    def far_row(l, carry):
        found = jnp.int32(0)
        parents = [jnp.int32(-1)] * REMOTE
        for c in range(low_count):
            parent = parent_low[l * low_count + c]
            away = lax.div(parent, mid_count) != l
            for s in range(REMOTE):
                parents[s] = jnp.where(away & (found == s), parent, parents[s])
            found = found + jnp.where(away, 1, 0)
        for s in range(REMOTE):
            far_parent[l * REMOTE + s] = parents[s]
        return carry

    lax.fori_loop(0, leaves, far_row, 0)
    found = jnp.int32(0)
    nodes = [jnp.int32(0)] * REMOTE
    for c in range(low_count):
        parent = parent_low[leaf * low_count + c]
        away = lax.div(parent, mid_count) != leaf
        for s in range(REMOTE):
            nodes[s] = jnp.where(away & (found == s), c, nodes[s])
        place[c] = jnp.where(
            away, mid_count + jnp.minimum(found, REMOTE - 1), lax.rem(parent, mid_count)
        )
        found = found + jnp.where(away, 1, 0)
    for s in range(REMOTE):
        far_index[s] = nodes[s]

    levels = lax.broadcasted_iota(jnp.int32, (emit_low.shape[1], images), 0)

    def picks(row):
        return jnp.where(levels == row, 1.0, 0.0).astype(jnp.bfloat16)

    def scale(inside):
        return jnp.exp(inside - jnp.max(inside, axis=0, keepdims=True))

    for load in loads[0:3]:
        load.wait()

    def message(node):
        inside = dot(emit_low[node], picks(pixels_low[pl.ds(node, 1), :]), 0, 0)
        scaled = scale(inside).astype(jnp.bfloat16)
        return jnp.log(dot(trans_low[node], scaled, 1, 0))

    def far(s, carry):
        far_up[s] = message(far_index[s])
        return carry

    lax.fori_loop(0, REMOTE, far, 0)
    mine = pl.ds(pl.multiple_of(part * images, images), images)
    loads[3].wait()
    pix[part, 0:low_count, :] = pixels_low[...]
    pix[part, low_count : low_count + mid_count, :] = pixels_mid[...]
    pl.semaphore_wait(barrier, devices - 1)
    each_part(lambda q: send(pix.at[part], pix.at[part], 0, leaf, q))
    each_other(
        lambda t, l, q: send(
            far_up.at[:, slice_of(l, q), :], far_slices.at[leaf, :, :, mine], 3, l, q
        )
    )
    far_slices[leaf, :, :, mine] = far_up[:, slice_of(leaf, part), :]
    for load in loads[4:7]:
        load.wait()
    own_top[...] = dot(emit_top[0], picks(pixels_top[...]), 0, 0) + outside_top[0].T
    each_near(
        lambda t, l, q: send(
            own_top.at[tall_slice_of(l, q)],
            edge_top.at[lax.rem(leaf, side), :, mine],
            1,
            l,
            q,
        )
    )
    edge_top[lax.rem(leaf, side), :, mine] = own_top[tall_slice_of(leaf, part), :]

    near_sums[...] = jnp.zeros(near_sums.shape, jnp.float32)

    def near(c, carry):
        up = message(c)
        for m in range(mid_count):
            parent = parent_low[leaf * low_count + c]
            weight = jnp.where(parent == leaf * mid_count + m, 1.0, 0.0)
            near_sums[m] += weight * up
        return carry

    lax.fori_loop(0, low_count, near, 0)
    each_part(lambda q: send(near_sums.at[q], inside_near.at[:, mine], 4, leaf, q))
    inside_near[:, mine] = near_sums[part]
    wait_recv(pix.at[pl.ds(0, parts - 1)], 0)

    def lookup(table, node):
        chosen = jnp.concatenate(
            [picks(pix[q, pl.ds(node, 1), :]) for q in range(parts)], axis=1
        )
        return dot(table, chosen, 0, 0)

    loads[7].wait()
    loads[8].wait()
    inside_own[...] = lookup(emit_mid[...], low_count + part)

    def whole(c, carry):
        scaled = scale(lookup(emit_low[c], c)).astype(jnp.bfloat16)
        scaled_low[c] = scaled
        linear_low[c] = dot(trans_low[c, quarter_of(part), :], scaled, 1, 0)
        return carry

    first, second = low_count * 3 // 5, low_count * 4 // 5
    lax.fori_loop(0, first, whole, 0)

    wait_recv(far_up.at[:, pl.ds(0, states - rows)], 3)

    def sum_far(t):
        total = jnp.zeros((rows, images * parts), jnp.float32)
        for l in range(leaves):
            for s in range(REMOTE):
                weight = jnp.where(far_parent[l * REMOTE + s] == t, 1.0, 0.0)
                total += weight * far_slices[l, s]
        return total

    def send_half(h, t, l, q):
        send(mid_send.at[h, t], mid_sums.at[h, slice_of(leaf, part)], 12 + h, l, q)

    def send_sum(t, l, q):
        total = sum_far(t)
        for h in range(HALVES):
            mid_send[h, t] = total[:, h * wide : (h + 1) * wide]
        send_half(0, t, l, q)

    each_other(send_sum)
    for h in range(1, HALVES):
        each_other(functools.partial(send_half, h))
    total = sum_far(me)
    for h in range(HALVES):
        mid_sums[h, slice_of(leaf, part), :] = total[:, h * wide : (h + 1) * wide]

    lax.fori_loop(first, second, whole, 0)
    wait_recv(near_sums.at[pl.ds(0, parts - 1)], 4)

    for h in range(HALVES):
        wait_recv(mid_sums.at[h, pl.ds(0, states - rows)], 12 + h)
        exact = scale(inside_own[:, lanes(h)] + inside_near[:, lanes(h)] + mid_sums[h])
        post_mid[h] = exact
        scaled = exact.astype(jnp.bfloat16)
        scaled_mid[:, lanes(h)] = scaled
        linear = dot(trans_mid[...], scaled, 1, 0)
        linear_mid[h] = linear
        up_mid[h] = jnp.log(linear)
        each_near(
            lambda t, l, q: send(
                up_mid.at[h, tall_slice_of(l, q)], up_slices.at[h, spot], 14 + h, l, q
            )
        )
        up_slices[h, spot] = up_mid[h, tall_slice_of(leaf, part), :]

    wait_recv(own_top.at[pl.ds(0, states - 2 * rows)], 1)
    for h in range(HALVES):
        wait_recv(up_slices.at[h, pl.ds(0, pairs - 1)], 14 + h)

        def top(r, carry):
            here = jnp.where(lax.div(r, side) == lax.div(leaf, side), 1.0, 0.0)
            total = here * edge_top[lax.rem(r, side), :, lanes(h)]
            for p in range(pairs):
                weight = jnp.where(parent_mid[base * parts + p] == r, 1.0, 0.0)
                total += weight * up_slices[h, p]
            partial_own[h, r] = total
            return carry

        lax.fori_loop(0, leaves, top, 0)
        send(partial_own.at[h], partial_far.at[h], 24 + h, lax.rem(leaf + side, leaves), part)

    for h in range(HALVES):
        wait_recv(partial_far.at[h], 24 + h)
        totals[h] = partial_own[h] + partial_far[h]

        def send_total(t, l, q):
            total_send[h, t] = totals[h, parent_mid[base * parts + t]]
            send(
                total_send.at[h, t], total_mine.at[h, tall_slice_of(leaf, part)], 16 + h, l, q
            )

        each_near(send_total)
        total_mine[h, tall_slice_of(leaf, part), :] = totals[h, parent_mid[me]]

    for h in range(HALVES):
        wait_recv(total_mine.at[h, pl.ds(0, states - 2 * rows)], 16 + h)
        reached = scale(total_mine[h])
        share = (
            reached / (linear_mid[h] * jnp.sum(reached, axis=0, keepdims=True))
        ).astype(jnp.bfloat16)
        share_mid[:, lanes(h)] = share
        posterior = post_mid[h] * dot(trans_mid[...], share, 0, 0)
        post_mid[h] = posterior / jnp.sum(posterior, axis=0, keepdims=True)
        each_other(
            lambda t, l, q: send(
                post_mid.at[h, slice_of(l, q)], post_slices[h].at[me], 18 + h, l, q
            )
        )
        post_slices[h][me] = post_mid[h, slice_of(leaf, part), :]
        each_part(
            lambda q: send(
                post_mid.at[h, quarter_of(q)], post_near.at[part, :, lanes(h)], 20 + h, leaf, q
            )
        )
        post_near[part, :, lanes(h)] = post_mid[h, quarter_of(part), :]

    def finished(share, scaled, weight):
        counts = dot(share, scaled, 1, 1) * weight.astype(jnp.float32) + PSEUDO
        return states * counts / jnp.sum(counts, axis=-1, keepdims=True)

    counts_own[...] = finished(share_mid[...], scaled_mid[...], trans_mid[...])
    each_part(lambda q: send(counts_own.at[quarter_of(q)], counts_mid.at[part], 2, leaf, q))
    counts_mid[part] = counts_own[quarter_of(part), :]

    lax.fori_loop(second, low_count, whole, 0)

    landing = pl.ds(pl.multiple_of(leaf * rows, rows), rows)
    for h in range(HALVES):
        wait_recv(post_slices[h].at[pl.ds(0, devices - 1)], 18 + h)

        def pick(l):
            for s in range(REMOTE):
                parent = jnp.maximum(far_parent[l * REMOTE + s], 0)
                post_send[h, l, s] = post_slices[h][parent]

        def send_pick(l):
            pick(l)
            send(
                post_send.at[h, l],
                post_far.at[:, landing, lanes(h)],
                22 + h,
                l,
                part,
            )

        each_leaf(send_pick)
        pick(leaf)
        post_far[:, landing, lanes(h)] = post_send[h, leaf]

    def update_of(c, found):
        share = (found / linear_low[c]).astype(jnp.bfloat16)
        return finished(share, scaled_low[c], trans_low[c, quarter_of(part), :])

    for h in range(HALVES):
        wait_recv(post_mid.at[h, pl.ds(0, states - share_rows)], 20 + h)

    def near_update(c, carry):
        update_low[c] = update_of(c, post_near[jnp.minimum(place[c], mid_count - 1)])
        return carry

    lax.fori_loop(0, low_count, near_update, 0)
    wait_recv(counts_mid.at[pl.ds(0, parts - 1)], 2)
    update_mid[...] = counts_mid[...]
    for h in range(HALVES):
        wait_recv(post_send.at[h, pl.ds(0, leaves - 1)], 22 + h)

    def far_update(s, carry):
        far_counts[s] = update_of(far_index[s], post_far[s])
        return carry

    lax.fori_loop(0, REMOTE, far_update, 0)

    def choose(c, carry):
        slot = place[c] - mid_count
        update_low[c] = jnp.where(
            slot >= 0, far_counts[jnp.maximum(slot, 0)], update_low[c]
        )
        return carry

    lax.fori_loop(0, low_count, choose, 0)

    wait_send(pix.at[pl.ds(0, parts - 1)], 0)
    wait_send(own_top.at[pl.ds(0, states - 2 * rows)], 1)
    wait_send(counts_mid.at[pl.ds(0, parts - 1)], 2)
    wait_send(far_up.at[:, pl.ds(0, states - rows)], 3)
    wait_send(near_sums.at[pl.ds(0, parts - 1)], 4)
    for h in range(HALVES):
        wait_send(mid_send.at[h, pl.ds(0, devices - 1)], 12 + h)
        wait_send(up_slices.at[h, pl.ds(0, pairs - 1)], 14 + h)
        wait_send(total_send.at[h, pl.ds(0, pairs - 1)], 16 + h)
        wait_send(partial_own.at[h], 24 + h)
        wait_send(post_slices[h].at[pl.ds(0, devices - 1)], 18 + h)
        wait_send(post_mid.at[h, pl.ds(0, states - share_rows)], 20 + h)
        wait_send(post_send.at[h, pl.ds(0, leaves - 1)], 22 + h)


def fused(
    leaves,
    parts,
    pixels_low,
    pixels_mid,
    pixels_top,
    emit_low,
    emit_mid,
    emit_top,
    trans_low,
    trans_mid,
    outside_top,
    parent_low,
    parent_mid,
):
    low_count, images = pixels_low.shape
    mid_count = pixels_mid.shape[0]
    states = trans_low.shape[2]
    devices = leaves * parts
    share_rows = states // parts
    rows = states // devices
    whole = images * parts
    wide = whole // HALVES
    held = -(-(low_count + mid_count) // 8) * 8
    real, half = jnp.float32, jnp.bfloat16
    vmem = pltpu.VMEM
    arrays = (pixels_low, pixels_mid, pixels_top, emit_low, emit_mid, emit_top, trans_low)
    arrays += (trans_mid, outside_top)
    return pl.pallas_call(
        functools.partial(kernel, leaves, parts),
        out_shape=(
            jax.ShapeDtypeStruct((low_count, share_rows, states), real),
            jax.ShapeDtypeStruct((mid_count, share_rows, states), real),
        ),
        in_specs=[pl.BlockSpec(memory_space=pltpu.SMEM)] * 2
        + [pl.BlockSpec(memory_space=pltpu.HBM)] * len(arrays),
        out_specs=(pl.BlockSpec(memory_space=pltpu.VMEM),) * 2,
        scratch_shapes=[
            pltpu.SMEM((REMOTE,), jnp.int32),
            pltpu.SMEM((leaves * REMOTE,), jnp.int32),
            pltpu.SMEM((low_count,), jnp.int32),
            vmem(pixels_low.shape, jnp.int32),
            vmem(pixels_mid.shape, jnp.int32),
            vmem(pixels_top.shape, jnp.int32),
            vmem(emit_low.shape, half),
            vmem(emit_mid.shape[1:], half),
            vmem(emit_top.shape, half),
            vmem(trans_low.shape, half),
            vmem(trans_mid.shape[1:], half),
            vmem(outside_top.shape, real),
            vmem((parts, held, images), jnp.int32),
            vmem((leaves // 2, 2 * rows, whole), real),
            vmem((states, images), real),
            vmem((REMOTE, states, images), real),
            vmem((leaves, REMOTE, rows, whole), real),
            vmem((HALVES, devices, rows, wide), real),
            vmem((HALVES, states, wide), real),
            vmem((states, whole), real),
            vmem((low_count, states, whole), half),
            vmem((low_count, share_rows, whole), real),
            vmem((mid_count, states, images), real),
            vmem((states, whole), real),
            vmem((HALVES, states, wide), real),
            vmem((HALVES, devices // 2, 2 * rows, wide), real),
            vmem((HALVES, leaves, 2 * rows, wide), real),
            vmem((HALVES, leaves, 2 * rows, wide), real),
            vmem((HALVES, leaves, 2 * rows, wide), real),
            vmem((HALVES, devices // 2, 2 * rows, wide), real),
            vmem((HALVES, states, wide), real),
            vmem((states, whole), half),
            vmem((HALVES, states, wide), real),
            vmem((states, whole), half),
            vmem((HALVES, states, wide), real),
            (vmem((devices, rows, wide), real),) * HALVES,
            vmem((HALVES, leaves, REMOTE, rows, wide), real),
            vmem((mid_count, share_rows, whole), real),
            vmem((REMOTE, share_rows, whole), real),
            vmem((mid_count, share_rows, states), real),
            vmem((states, states), real),
            vmem((REMOTE, share_rows, states), real),
            pltpu.SemaphoreType.DMA((26,)),
            pltpu.SemaphoreType.DMA((26,)),
            pltpu.SemaphoreType.DMA((len(arrays),)),
        ],
        compiler_params=pltpu.CompilerParams(
            collective_id=0, has_side_effects=True, vmem_limit_bytes=62 * 2**20
        ),
    )(parent_low, parent_mid, *arrays)


def solution(mesh):
    leaves, parts = mesh.shape["leaf"], mesh.shape["batch"]
    fits = leaves % 2 == 0 and 256 % (8 * leaves * parts) == 0
    chosen = functools.partial(fused, leaves, parts) if fits else body
    return jax.shard_map(
        chosen,
        mesh=mesh,
        in_specs=(
            P("leaf", "batch"),
            P("leaf", "batch"),
            P("leaf", "batch"),
            P("leaf", None, None),
            P("leaf", None, None),
            P("leaf", None, None),
            P("leaf", None, None),
            P("leaf", None, None),
            P("leaf", "batch", None),
            P(),
            P(),
        ),
        out_specs=(P("leaf", "batch", None), P("leaf", "batch", None)),
        check_vma=False,
    )
```

```python
import functools

import jax
import jax.numpy as jnp
from jax import lax
from jax.experimental import pallas as pl
from jax.experimental.pallas import tpu as pltpu
from jax.sharding import PartitionSpec as P

PSEUDO = 0.001
REMOTE = 3
HALVES = 2
STRIDE = 13
MESH = pl.DeviceIdType.MESH


def lookup_all(table, pixels):
    levels = jnp.arange(table.shape[1], dtype=jnp.int32)
    picks = (pixels[:, :, None] == levels[None, None, :]).astype(jnp.bfloat16)
    return jnp.einsum("nbv,nvk->nbk", picks, table, preferred_element_type=jnp.float32)


def upward_all(inside, weight):
    top = jnp.max(inside, axis=-1, keepdims=True)
    scaled = jnp.exp(inside - top).astype(jnp.bfloat16)
    linear = jnp.einsum("nbj,nij->nbi", scaled, weight, preferred_element_type=jnp.float32)
    return (jnp.log(linear) + top, scaled)


def edge_all(above, weight, scaled):
    peak = jnp.max(above, axis=-1, keepdims=True)
    pushed = jnp.exp(above - peak).astype(jnp.bfloat16)
    reach = jnp.einsum("nbi,nij->nbj", pushed, weight, preferred_element_type=jnp.float32)
    total = jnp.sum(reach * scaled.astype(jnp.float32), axis=-1, keepdims=True)
    share = (pushed.astype(jnp.float32) / total).astype(jnp.bfloat16)
    counts = jnp.einsum("nbi,nbj->nij", share, scaled, preferred_element_type=jnp.float32)
    return (counts * weight.astype(jnp.float32), jnp.log(reach) + peak)


def finish(summed):
    counts = summed + PSEUDO
    return counts.shape[-1] * counts / jnp.sum(counts, axis=-1, keepdims=True)


def body(
    pixels_low,
    pixels_mid,
    pixels_top,
    emit_low,
    emit_mid,
    emit_top,
    trans_low,
    trans_mid,
    outside_top,
    parent_low,
    parent_mid,
):
    devices = lax.axis_size("leaf")
    mid_count = emit_mid.shape[0]
    top_count = emit_top.shape[0]
    up_low, scaled_low = upward_all(lookup_all(emit_low, pixels_low), trans_low)
    emis_mid = lookup_all(emit_mid, pixels_mid)
    emis_top = lookup_all(emit_top, pixels_top)
    moved = lax.all_to_all(up_low, "leaf", split_axis=1, concat_axis=0, tiled=True)
    gathered_mid = jax.ops.segment_sum(moved, parent_low, num_segments=mid_count * devices)
    sums_mid = lax.all_to_all(gathered_mid, "leaf", split_axis=0, concat_axis=1, tiled=True)
    inside_mid = emis_mid + sums_mid
    up_mid, scaled_mid = upward_all(inside_mid, trans_mid)
    moved_mid = lax.all_to_all(up_mid, "leaf", split_axis=1, concat_axis=0, tiled=True)
    gathered_top = jax.ops.segment_sum(moved_mid, parent_mid, num_segments=top_count * devices)
    sums_top = lax.all_to_all(gathered_top, "leaf", split_axis=0, concat_axis=1, tiled=True)
    total_top = emis_top + sums_top + outside_top
    spread_top = lax.all_to_all(total_top, "leaf", split_axis=1, concat_axis=0, tiled=True)
    picked = lax.all_to_all(spread_top[parent_mid], "leaf", split_axis=0, concat_axis=1, tiled=True)
    counts_mid, outside_mid = edge_all(picked - up_mid, trans_mid, scaled_mid)
    update_mid = finish(lax.psum_scatter(counts_mid, "batch", scatter_dimension=1, tiled=True))
    total_mid = inside_mid + outside_mid
    spread_mid = lax.all_to_all(total_mid, "leaf", split_axis=1, concat_axis=0, tiled=True)
    above_low = lax.all_to_all(
        spread_mid[parent_low], "leaf", split_axis=0, concat_axis=1, tiled=True
    )
    counts_low, unused = edge_all(above_low - up_low, trans_low, scaled_low)
    update_low = finish(lax.psum_scatter(counts_low, "batch", scatter_dimension=1, tiled=True))
    return (update_low, update_mid)


def dot(a, b, left, right):
    return lax.dot_general(
        a, b, (((left,), (right,)), ((), ())), preferred_element_type=jnp.float32
    )


def kernel(
    leaves,
    parts,
    parent_low,
    parent_mid,
    pixels_low_hbm,
    pixels_mid_hbm,
    pixels_top_hbm,
    emit_low_hbm,
    emit_mid_hbm,
    emit_top_hbm,
    trans_low_hbm,
    trans_mid_hbm,
    outside_top_hbm,
    update_low,
    update_mid,
    far_index,
    far_parent,
    place,
    pixels_low,
    pixels_mid,
    pixels_top,
    emit_low,
    emit_mid,
    emit_top,
    trans_low,
    trans_mid,
    outside_top,
    pix,
    edge_top,
    own_top,
    far_up,
    far_slices,
    mid_send,
    mid_sums,
    inside_own,
    scaled_low,
    linear_low,
    near_sums,
    inside_near,
    up_mid,
    up_slices,
    totals,
    total_send,
    total_mine,
    scaled_mid,
    linear_mid,
    share_mid,
    post_mid,
    post_slices,
    post_send,
    post_near,
    post_far,
    counts_mid,
    counts_own,
    far_counts,
    send_sem,
    recv_sem,
    load_sem,
):
    leaf = lax.axis_index("leaf")
    part = lax.axis_index("batch")
    devices = leaves * parts
    me = leaf * parts + part
    low_count = pixels_low.shape[0]
    mid_count = pixels_mid.shape[0]
    images = pixels_low.shape[1]
    states = trans_low.shape[2]
    share_rows = states // parts
    rows = states // devices
    wide = images * parts // HALVES

    loads = [
        pltpu.make_async_copy(source, target, load_sem.at[i])
        for i, (source, target) in enumerate(
            (
                (pixels_low_hbm, pixels_low),
                (emit_low_hbm, emit_low),
                (trans_low_hbm, trans_low),
                (pixels_mid_hbm, pixels_mid),
                (pixels_top_hbm, pixels_top),
                (emit_top_hbm, emit_top),
                (outside_top_hbm, outside_top),
                (emit_mid_hbm.at[part], emit_mid),
                (trans_mid_hbm.at[part], trans_mid),
            )
        )
    ]
    for load in loads:
        load.start()

    def slice_of(l, q):
        return pl.ds(pl.multiple_of(q * share_rows + l * rows, rows), rows)

    def quarter_of(q):
        return pl.ds(pl.multiple_of(q * share_rows, share_rows), share_rows)

    def lanes(h):
        return pl.ds(h * wide, wide)

    def send(src, dst, phase, l, q):
        pltpu.make_async_remote_copy(
            src_ref=src,
            dst_ref=dst,
            send_sem=send_sem.at[phase],
            recv_sem=recv_sem.at[phase],
            device_id=(l, q),
            device_id_type=MESH,
        ).start()

    def wait_recv(ref, phase):
        pltpu.make_async_copy(ref, ref, recv_sem.at[phase]).wait()

    def wait_send(ref, phase):
        pltpu.make_async_copy(ref, ref, send_sem.at[phase]).wait()

    def each_other(step):
        def one(k, carry):
            t = lax.rem(me + STRIDE * k, devices)
            step(t, lax.div(t, parts), lax.rem(t, parts))
            return carry

        lax.fori_loop(1, devices, one, 0)

    def each_leaf(step):
        def one(k, carry):
            step(lax.rem(leaf + 3 * k, leaves))
            return carry

        lax.fori_loop(1, leaves, one, 0)

    def each_part(step):
        def one(k, carry):
            step(lax.rem(part + k, parts))
            return carry

        lax.fori_loop(1, parts, one, 0)

    barrier = pltpu.get_barrier_semaphore()

    def greet(t, l, q):
        pl.semaphore_signal(barrier, inc=1, device_id=(l, q), device_id_type=MESH)

    each_other(greet)

    def far_row(l, carry):
        found = jnp.int32(0)
        parents = [jnp.int32(-1)] * REMOTE
        for c in range(low_count):
            parent = parent_low[l * low_count + c]
            away = lax.div(parent, mid_count) != l
            for s in range(REMOTE):
                parents[s] = jnp.where(away & (found == s), parent, parents[s])
            found = found + jnp.where(away, 1, 0)
        for s in range(REMOTE):
            far_parent[l * REMOTE + s] = parents[s]
        return carry

    lax.fori_loop(0, leaves, far_row, 0)
    found = jnp.int32(0)
    nodes = [jnp.int32(0)] * REMOTE
    for c in range(low_count):
        parent = parent_low[leaf * low_count + c]
        away = lax.div(parent, mid_count) != leaf
        for s in range(REMOTE):
            nodes[s] = jnp.where(away & (found == s), c, nodes[s])
        place[c] = jnp.where(
            away, mid_count + jnp.minimum(found, REMOTE - 1), lax.rem(parent, mid_count)
        )
        found = found + jnp.where(away, 1, 0)
    for s in range(REMOTE):
        far_index[s] = nodes[s]

    levels = lax.broadcasted_iota(jnp.int32, (emit_low.shape[1], images), 0)

    def picks(row):
        return jnp.where(levels == row, 1.0, 0.0).astype(jnp.bfloat16)

    def scale(inside):
        return jnp.exp(inside - jnp.max(inside, axis=0, keepdims=True))

    for load in loads[0:3]:
        load.wait()

    def message(node):
        inside = dot(emit_low[node], picks(pixels_low[pl.ds(node, 1), :]), 0, 0)
        scaled = scale(inside).astype(jnp.bfloat16)
        return jnp.log(dot(trans_low[node], scaled, 1, 0))

    def far(s, carry):
        far_up[s] = message(far_index[s])
        return carry

    lax.fori_loop(0, REMOTE, far, 0)
    mine = pl.ds(pl.multiple_of(part * images, images), images)
    loads[3].wait()
    pix[part, 0:low_count, :] = pixels_low[...]
    pix[part, low_count : low_count + mid_count, :] = pixels_mid[...]
    pl.semaphore_wait(barrier, devices - 1)
    each_part(lambda q: send(pix.at[part], pix.at[part], 0, leaf, q))
    each_other(
        lambda t, l, q: send(
            far_up.at[:, slice_of(l, q), :], far_slices.at[leaf, :, :, mine], 3, l, q
        )
    )
    far_slices[leaf, :, :, mine] = far_up[:, slice_of(leaf, part), :]
    for load in loads[4:7]:
        load.wait()
    own_top[...] = dot(emit_top[0], picks(pixels_top[...]), 0, 0) + outside_top[0].T
    each_other(
        lambda t, l, q: send(
            own_top.at[slice_of(l, q)], edge_top.at[leaf, :, mine], 1, l, q
        )
    )
    edge_top[leaf, :, mine] = own_top[slice_of(leaf, part), :]

    near_sums[...] = jnp.zeros(near_sums.shape, jnp.float32)

    def near(c, carry):
        up = message(c)
        for m in range(mid_count):
            parent = parent_low[leaf * low_count + c]
            weight = jnp.where(parent == leaf * mid_count + m, 1.0, 0.0)
            near_sums[m] += weight * up
        return carry

    lax.fori_loop(0, low_count, near, 0)
    each_part(lambda q: send(near_sums.at[q], inside_near.at[:, mine], 4, leaf, q))
    inside_near[:, mine] = near_sums[part]
    wait_recv(pix.at[pl.ds(0, parts - 1)], 0)

    def lookup(table, node):
        chosen = jnp.concatenate(
            [picks(pix[q, pl.ds(node, 1), :]) for q in range(parts)], axis=1
        )
        return dot(table, chosen, 0, 0)

    loads[7].wait()
    loads[8].wait()
    inside_own[...] = lookup(emit_mid[...], low_count + part)

    def whole(c, carry):
        scaled = scale(lookup(emit_low[c], c)).astype(jnp.bfloat16)
        scaled_low[c] = scaled
        linear_low[c] = dot(trans_low[c, quarter_of(part), :], scaled, 1, 0)
        return carry

    first, second = low_count * 3 // 5, low_count * 4 // 5
    lax.fori_loop(0, first, whole, 0)

    wait_recv(far_up.at[:, pl.ds(0, states - rows)], 3)

    def sum_far(t):
        total = jnp.zeros((rows, images * parts), jnp.float32)
        for l in range(leaves):
            for s in range(REMOTE):
                weight = jnp.where(far_parent[l * REMOTE + s] == t, 1.0, 0.0)
                total += weight * far_slices[l, s]
        return total

    def send_half(h, t, l, q):
        send(mid_send.at[h, t], mid_sums.at[h, slice_of(leaf, part)], 12 + h, l, q)

    def send_sum(t, l, q):
        total = sum_far(t)
        for h in range(HALVES):
            mid_send[h, t] = total[:, h * wide : (h + 1) * wide]
        send_half(0, t, l, q)

    each_other(send_sum)
    for h in range(1, HALVES):
        each_other(functools.partial(send_half, h))
    total = sum_far(me)
    for h in range(HALVES):
        mid_sums[h, slice_of(leaf, part), :] = total[:, h * wide : (h + 1) * wide]

    lax.fori_loop(first, second, whole, 0)
    wait_recv(near_sums.at[pl.ds(0, parts - 1)], 4)

    for h in range(HALVES):
        wait_recv(mid_sums.at[h, pl.ds(0, states - rows)], 12 + h)
        exact = scale(inside_own[:, lanes(h)] + inside_near[:, lanes(h)] + mid_sums[h])
        post_mid[h] = exact
        scaled = exact.astype(jnp.bfloat16)
        scaled_mid[:, lanes(h)] = scaled
        linear = dot(trans_mid[...], scaled, 1, 0)
        linear_mid[h] = linear
        up_mid[h] = jnp.log(linear)
        each_other(
            lambda t, l, q: send(
                up_mid.at[h, slice_of(l, q)], up_slices.at[h, me], 14 + h, l, q
            )
        )
        up_slices[h, me] = up_mid[h, slice_of(leaf, part), :]

    wait_recv(own_top.at[pl.ds(0, states - rows)], 1)
    for h in range(HALVES):
        wait_recv(up_slices.at[h, pl.ds(0, devices - 1)], 14 + h)

        def top(r, carry):
            total = edge_top[r, :, lanes(h)]
            for p in range(devices):
                weight = jnp.where(parent_mid[p] == r, 1.0, 0.0)
                total += weight * up_slices[h, p]
            totals[h, r] = total
            return carry

        lax.fori_loop(0, leaves, top, 0)

        def send_total(t, l, q):
            total_send[h, t] = totals[h, parent_mid[t]]
            send(total_send.at[h, t], total_mine.at[h, slice_of(leaf, part)], 16 + h, l, q)

        each_other(send_total)
        total_mine[h, slice_of(leaf, part), :] = totals[h, parent_mid[me]]

    for h in range(HALVES):
        wait_recv(total_mine.at[h, pl.ds(0, states - rows)], 16 + h)
        reached = scale(total_mine[h])
        share = (
            reached / (linear_mid[h] * jnp.sum(reached, axis=0, keepdims=True))
        ).astype(jnp.bfloat16)
        share_mid[:, lanes(h)] = share
        posterior = post_mid[h] * dot(trans_mid[...], share, 0, 0)
        post_mid[h] = posterior / jnp.sum(posterior, axis=0, keepdims=True)
        each_other(
            lambda t, l, q: send(
                post_mid.at[h, slice_of(l, q)], post_slices[h].at[me], 18 + h, l, q
            )
        )
        post_slices[h][me] = post_mid[h, slice_of(leaf, part), :]
        each_part(
            lambda q: send(
                post_mid.at[h, quarter_of(q)], post_near.at[part, :, lanes(h)], 20 + h, leaf, q
            )
        )
        post_near[part, :, lanes(h)] = post_mid[h, quarter_of(part), :]

    def finished(share, scaled, weight):
        counts = dot(share, scaled, 1, 1) * weight.astype(jnp.float32) + PSEUDO
        return states * counts / jnp.sum(counts, axis=-1, keepdims=True)

    counts_own[...] = finished(share_mid[...], scaled_mid[...], trans_mid[...])
    each_part(lambda q: send(counts_own.at[quarter_of(q)], counts_mid.at[part], 2, leaf, q))
    counts_mid[part] = counts_own[quarter_of(part), :]

    lax.fori_loop(second, low_count, whole, 0)

    landing = pl.ds(pl.multiple_of(leaf * rows, rows), rows)
    for h in range(HALVES):
        wait_recv(post_slices[h].at[pl.ds(0, devices - 1)], 18 + h)

        def pick(l):
            for s in range(REMOTE):
                parent = jnp.maximum(far_parent[l * REMOTE + s], 0)
                post_send[h, l, s] = post_slices[h][parent]

        def send_pick(l):
            pick(l)
            send(
                post_send.at[h, l],
                post_far.at[:, landing, lanes(h)],
                22 + h,
                l,
                part,
            )

        each_leaf(send_pick)
        pick(leaf)
        post_far[:, landing, lanes(h)] = post_send[h, leaf]

    def update_of(c, found):
        share = (found / linear_low[c]).astype(jnp.bfloat16)
        return finished(share, scaled_low[c], trans_low[c, quarter_of(part), :])

    for h in range(HALVES):
        wait_recv(post_mid.at[h, pl.ds(0, states - share_rows)], 20 + h)

    def near_update(c, carry):
        update_low[c] = update_of(c, post_near[jnp.minimum(place[c], mid_count - 1)])
        return carry

    lax.fori_loop(0, low_count, near_update, 0)
    wait_recv(counts_mid.at[pl.ds(0, parts - 1)], 2)
    update_mid[...] = counts_mid[...]
    for h in range(HALVES):
        wait_recv(post_send.at[h, pl.ds(0, leaves - 1)], 22 + h)

    def far_update(s, carry):
        far_counts[s] = update_of(far_index[s], post_far[s])
        return carry

    lax.fori_loop(0, REMOTE, far_update, 0)

    def choose(c, carry):
        slot = place[c] - mid_count
        update_low[c] = jnp.where(
            slot >= 0, far_counts[jnp.maximum(slot, 0)], update_low[c]
        )
        return carry

    lax.fori_loop(0, low_count, choose, 0)

    wait_send(pix.at[pl.ds(0, parts - 1)], 0)
    wait_send(own_top.at[pl.ds(0, states - rows)], 1)
    wait_send(counts_mid.at[pl.ds(0, parts - 1)], 2)
    wait_send(far_up.at[:, pl.ds(0, states - rows)], 3)
    wait_send(near_sums.at[pl.ds(0, parts - 1)], 4)
    for h in range(HALVES):
        wait_send(mid_send.at[h, pl.ds(0, devices - 1)], 12 + h)
        wait_send(up_slices.at[h, pl.ds(0, devices - 1)], 14 + h)
        wait_send(total_send.at[h, pl.ds(0, devices - 1)], 16 + h)
        wait_send(post_slices[h].at[pl.ds(0, devices - 1)], 18 + h)
        wait_send(post_mid.at[h, pl.ds(0, states - share_rows)], 20 + h)
        wait_send(post_send.at[h, pl.ds(0, leaves - 1)], 22 + h)


def fused(
    leaves,
    parts,
    pixels_low,
    pixels_mid,
    pixels_top,
    emit_low,
    emit_mid,
    emit_top,
    trans_low,
    trans_mid,
    outside_top,
    parent_low,
    parent_mid,
):
    low_count, images = pixels_low.shape
    mid_count = pixels_mid.shape[0]
    states = trans_low.shape[2]
    devices = leaves * parts
    share_rows = states // parts
    rows = states // devices
    whole = images * parts
    wide = whole // HALVES
    held = -(-(low_count + mid_count) // 8) * 8
    real, half = jnp.float32, jnp.bfloat16
    vmem = pltpu.VMEM
    arrays = (pixels_low, pixels_mid, pixels_top, emit_low, emit_mid, emit_top, trans_low)
    arrays += (trans_mid, outside_top)
    return pl.pallas_call(
        functools.partial(kernel, leaves, parts),
        out_shape=(
            vmem((low_count, share_rows, states), real),
            vmem((mid_count, share_rows, states), real),
        ),
        in_specs=[pl.BlockSpec(memory_space=pltpu.SMEM)] * 2
        + [pl.BlockSpec(memory_space=pltpu.HBM)] * len(arrays),
        out_specs=(pl.BlockSpec(memory_space=pltpu.VMEM),) * 2,
        scratch_shapes=[
            pltpu.SMEM((REMOTE,), jnp.int32),
            pltpu.SMEM((leaves * REMOTE,), jnp.int32),
            pltpu.SMEM((low_count,), jnp.int32),
            vmem(pixels_low.shape, jnp.int32),
            vmem(pixels_mid.shape, jnp.int32),
            vmem(pixels_top.shape, jnp.int32),
            vmem(emit_low.shape, half),
            vmem(emit_mid.shape[1:], half),
            vmem(emit_top.shape, half),
            vmem(trans_low.shape, half),
            vmem(trans_mid.shape[1:], half),
            vmem(outside_top.shape, real),
            vmem((parts, held, images), jnp.int32),
            vmem((leaves, rows, whole), real),
            vmem((states, images), real),
            vmem((REMOTE, states, images), real),
            vmem((leaves, REMOTE, rows, whole), real),
            vmem((HALVES, devices, rows, wide), real),
            vmem((HALVES, states, wide), real),
            vmem((states, whole), real),
            vmem((low_count, states, whole), half),
            vmem((low_count, share_rows, whole), real),
            vmem((mid_count, states, images), real),
            vmem((states, whole), real),
            vmem((HALVES, states, wide), real),
            vmem((HALVES, devices, rows, wide), real),
            vmem((HALVES, leaves, rows, wide), real),
            vmem((HALVES, devices, rows, wide), real),
            vmem((HALVES, states, wide), real),
            vmem((states, whole), half),
            vmem((HALVES, states, wide), real),
            vmem((states, whole), half),
            vmem((HALVES, states, wide), real),
            (vmem((devices, rows, wide), real),) * HALVES,
            vmem((HALVES, leaves, REMOTE, rows, wide), real),
            vmem((mid_count, share_rows, whole), real),
            vmem((REMOTE, share_rows, whole), real),
            vmem((mid_count, share_rows, states), real),
            vmem((states, states), real),
            vmem((REMOTE, share_rows, states), real),
            pltpu.SemaphoreType.DMA((24,)),
            pltpu.SemaphoreType.DMA((24,)),
            pltpu.SemaphoreType.DMA((len(arrays),)),
        ],
        compiler_params=pltpu.CompilerParams(
            collective_id=0, has_side_effects=True, vmem_limit_bytes=62 * 2**20
        ),
    )(parent_low, parent_mid, *arrays)


def solution(mesh):
    leaves, parts = mesh.shape["leaf"], mesh.shape["batch"]
    fits = 256 % (8 * leaves * parts) == 0
    chosen = functools.partial(fused, leaves, parts) if fits else body
    return jax.shard_map(
        chosen,
        mesh=mesh,
        in_specs=(
            P("leaf", "batch"),
            P("leaf", "batch"),
            P("leaf", "batch"),
            P("leaf", None, None),
            P("leaf", None, None),
            P("leaf", None, None),
            P("leaf", None, None),
            P("leaf", None, None),
            P("leaf", "batch", None),
            P(),
            P(),
        ),
        out_specs=(P("leaf", "batch", None), P("leaf", "batch", None)),
        check_vma=False,
    )
```

```python
import functools

import jax
import jax.numpy as jnp
from jax import lax
from jax.experimental import pallas as pl
from jax.experimental.pallas import tpu as pltpu
from jax.sharding import PartitionSpec as P

PSEUDO = 0.001
REMOTE = 3
HALVES = 2
STRIDE = 13
MESH = pl.DeviceIdType.MESH


def lookup_all(table, pixels):
    levels = jnp.arange(table.shape[1], dtype=jnp.int32)
    picks = (pixels[:, :, None] == levels[None, None, :]).astype(jnp.bfloat16)
    return jnp.einsum("nbv,nvk->nbk", picks, table, preferred_element_type=jnp.float32)


def upward_all(inside, weight):
    top = jnp.max(inside, axis=-1, keepdims=True)
    scaled = jnp.exp(inside - top).astype(jnp.bfloat16)
    linear = jnp.einsum("nbj,nij->nbi", scaled, weight, preferred_element_type=jnp.float32)
    return (jnp.log(linear) + top, scaled)


def edge_all(above, weight, scaled):
    peak = jnp.max(above, axis=-1, keepdims=True)
    pushed = jnp.exp(above - peak).astype(jnp.bfloat16)
    reach = jnp.einsum("nbi,nij->nbj", pushed, weight, preferred_element_type=jnp.float32)
    total = jnp.sum(reach * scaled.astype(jnp.float32), axis=-1, keepdims=True)
    share = (pushed.astype(jnp.float32) / total).astype(jnp.bfloat16)
    counts = jnp.einsum("nbi,nbj->nij", share, scaled, preferred_element_type=jnp.float32)
    return (counts * weight.astype(jnp.float32), jnp.log(reach) + peak)


def finish(summed):
    counts = summed + PSEUDO
    return counts.shape[-1] * counts / jnp.sum(counts, axis=-1, keepdims=True)


def body(
    pixels_low,
    pixels_mid,
    pixels_top,
    emit_low,
    emit_mid,
    emit_top,
    trans_low,
    trans_mid,
    outside_top,
    parent_low,
    parent_mid,
):
    devices = lax.axis_size("leaf")
    mid_count = emit_mid.shape[0]
    top_count = emit_top.shape[0]
    up_low, scaled_low = upward_all(lookup_all(emit_low, pixels_low), trans_low)
    emis_mid = lookup_all(emit_mid, pixels_mid)
    emis_top = lookup_all(emit_top, pixels_top)
    moved = lax.all_to_all(up_low, "leaf", split_axis=1, concat_axis=0, tiled=True)
    gathered_mid = jax.ops.segment_sum(moved, parent_low, num_segments=mid_count * devices)
    sums_mid = lax.all_to_all(gathered_mid, "leaf", split_axis=0, concat_axis=1, tiled=True)
    inside_mid = emis_mid + sums_mid
    up_mid, scaled_mid = upward_all(inside_mid, trans_mid)
    moved_mid = lax.all_to_all(up_mid, "leaf", split_axis=1, concat_axis=0, tiled=True)
    gathered_top = jax.ops.segment_sum(moved_mid, parent_mid, num_segments=top_count * devices)
    sums_top = lax.all_to_all(gathered_top, "leaf", split_axis=0, concat_axis=1, tiled=True)
    total_top = emis_top + sums_top + outside_top
    spread_top = lax.all_to_all(total_top, "leaf", split_axis=1, concat_axis=0, tiled=True)
    picked = lax.all_to_all(spread_top[parent_mid], "leaf", split_axis=0, concat_axis=1, tiled=True)
    counts_mid, outside_mid = edge_all(picked - up_mid, trans_mid, scaled_mid)
    update_mid = finish(lax.psum_scatter(counts_mid, "batch", scatter_dimension=1, tiled=True))
    total_mid = inside_mid + outside_mid
    spread_mid = lax.all_to_all(total_mid, "leaf", split_axis=1, concat_axis=0, tiled=True)
    above_low = lax.all_to_all(
        spread_mid[parent_low], "leaf", split_axis=0, concat_axis=1, tiled=True
    )
    counts_low, unused = edge_all(above_low - up_low, trans_low, scaled_low)
    update_low = finish(lax.psum_scatter(counts_low, "batch", scatter_dimension=1, tiled=True))
    return (update_low, update_mid)


def dot(a, b, left, right):
    return lax.dot_general(
        a, b, (((left,), (right,)), ((), ())), preferred_element_type=jnp.float32
    )


def kernel(
    leaves,
    parts,
    parent_low,
    parent_mid,
    pixels_low_hbm,
    pixels_mid_hbm,
    pixels_top_hbm,
    emit_low_hbm,
    emit_mid_hbm,
    emit_top_hbm,
    trans_low_hbm,
    trans_mid_hbm,
    outside_top_hbm,
    update_low,
    update_mid,
    far_index,
    far_parent,
    place,
    pixels_low,
    pixels_mid,
    pixels_top,
    emit_low,
    emit_mid,
    emit_top,
    trans_low,
    trans_mid,
    outside_top,
    pix,
    edge_top,
    own_top,
    far_up,
    far_slices,
    mid_send,
    mid_sums,
    inside_own,
    scaled_low,
    linear_low,
    linear_full,
    up_mid,
    up_slices,
    totals,
    total_send,
    total_mine,
    scaled_mid,
    linear_mid,
    share_mid,
    post_mid,
    post_slices,
    post_send,
    post_near,
    post_far,
    counts_mid,
    counts_own,
    far_counts,
    send_sem,
    recv_sem,
    load_sem,
):
    leaf = lax.axis_index("leaf")
    part = lax.axis_index("batch")
    devices = leaves * parts
    me = leaf * parts + part
    low_count = pixels_low.shape[0]
    mid_count = pixels_mid.shape[0]
    images = pixels_low.shape[1]
    states = trans_low.shape[2]
    share_rows = states // parts
    rows = states // devices
    wide = images * parts // HALVES

    loads = [
        pltpu.make_async_copy(source, target, load_sem.at[i])
        for i, (source, target) in enumerate(
            (
                (pixels_low_hbm, pixels_low),
                (emit_low_hbm, emit_low),
                (trans_low_hbm, trans_low),
                (pixels_mid_hbm, pixels_mid),
                (pixels_top_hbm, pixels_top),
                (emit_top_hbm, emit_top),
                (outside_top_hbm, outside_top),
                (emit_mid_hbm.at[part], emit_mid),
                (trans_mid_hbm.at[part], trans_mid),
            )
        )
    ]
    for load in loads:
        load.start()

    def slice_of(l, q):
        return pl.ds(pl.multiple_of(q * share_rows + l * rows, rows), rows)

    def quarter_of(q):
        return pl.ds(pl.multiple_of(q * share_rows, share_rows), share_rows)

    def lanes(h):
        return pl.ds(h * wide, wide)

    def send(src, dst, phase, l, q):
        pltpu.make_async_remote_copy(
            src_ref=src,
            dst_ref=dst,
            send_sem=send_sem.at[phase],
            recv_sem=recv_sem.at[phase],
            device_id=(l, q),
            device_id_type=MESH,
        ).start()

    def wait_recv(ref, phase):
        pltpu.make_async_copy(ref, ref, recv_sem.at[phase]).wait()

    def wait_send(ref, phase):
        pltpu.make_async_copy(ref, ref, send_sem.at[phase]).wait()

    def each_other(step):
        def one(k, carry):
            t = lax.rem(me + STRIDE * k, devices)
            step(t, lax.div(t, parts), lax.rem(t, parts))
            return carry

        lax.fori_loop(1, devices, one, 0)

    def each_leaf(step):
        def one(k, carry):
            step(lax.rem(leaf + 3 * k, leaves))
            return carry

        lax.fori_loop(1, leaves, one, 0)

    def each_part(step):
        def one(k, carry):
            step(lax.rem(part + k, parts))
            return carry

        lax.fori_loop(1, parts, one, 0)

    barrier = pltpu.get_barrier_semaphore()

    def greet(t, l, q):
        pl.semaphore_signal(barrier, inc=1, device_id=(l, q), device_id_type=MESH)

    each_other(greet)

    def far_row(l, carry):
        found = jnp.int32(0)
        parents = [jnp.int32(-1)] * REMOTE
        for c in range(low_count):
            parent = parent_low[l * low_count + c]
            away = lax.div(parent, mid_count) != l
            for s in range(REMOTE):
                parents[s] = jnp.where(away & (found == s), parent, parents[s])
            found = found + jnp.where(away, 1, 0)
        for s in range(REMOTE):
            far_parent[l * REMOTE + s] = parents[s]
        return carry

    lax.fori_loop(0, leaves, far_row, 0)
    found = jnp.int32(0)
    nodes = [jnp.int32(0)] * REMOTE
    for c in range(low_count):
        parent = parent_low[leaf * low_count + c]
        away = lax.div(parent, mid_count) != leaf
        for s in range(REMOTE):
            nodes[s] = jnp.where(away & (found == s), c, nodes[s])
        place[c] = jnp.where(
            away, mid_count + jnp.minimum(found, REMOTE - 1), lax.rem(parent, mid_count)
        )
        found = found + jnp.where(away, 1, 0)
    for s in range(REMOTE):
        far_index[s] = nodes[s]

    levels = lax.broadcasted_iota(jnp.int32, (emit_low.shape[1], images), 0)

    def picks(row):
        return jnp.where(levels == row, 1.0, 0.0).astype(jnp.bfloat16)

    def scale(inside):
        return jnp.exp(inside - jnp.max(inside, axis=0, keepdims=True))

    for load in loads[0:3]:
        load.wait()

    def message(node):
        inside = dot(emit_low[node], picks(pixels_low[pl.ds(node, 1), :]), 0, 0)
        scaled = scale(inside).astype(jnp.bfloat16)
        return jnp.log(dot(trans_low[node], scaled, 1, 0))

    def far(s, carry):
        far_up[s] = message(far_index[s])
        return carry

    lax.fori_loop(0, REMOTE, far, 0)
    mine = pl.ds(pl.multiple_of(part * images, images), images)
    loads[3].wait()
    pix[part, 0:low_count, :] = pixels_low[...]
    pix[part, low_count : low_count + mid_count, :] = pixels_mid[...]
    pl.semaphore_wait(barrier, devices - 1)
    each_part(lambda q: send(pix.at[part], pix.at[part], 0, leaf, q))
    each_other(
        lambda t, l, q: send(
            far_up.at[:, slice_of(l, q), :], far_slices.at[leaf, :, :, mine], 3, l, q
        )
    )
    far_slices[leaf, :, :, mine] = far_up[:, slice_of(leaf, part), :]
    for load in loads[4:7]:
        load.wait()
    own_top[...] = dot(emit_top[0], picks(pixels_top[...]), 0, 0) + outside_top[0].T
    each_other(
        lambda t, l, q: send(
            own_top.at[slice_of(l, q)], edge_top.at[leaf, :, mine], 1, l, q
        )
    )
    edge_top[leaf, :, mine] = own_top[slice_of(leaf, part), :]
    wait_recv(pix.at[pl.ds(0, parts - 1)], 0)

    def lookup(table, node):
        chosen = jnp.concatenate(
            [picks(pix[q, pl.ds(node, 1), :]) for q in range(parts)], axis=1
        )
        return dot(table, chosen, 0, 0)

    loads[7].wait()
    loads[8].wait()
    inside_own[...] = lookup(emit_mid[...], low_count + part)

    def near(c, carry):
        scaled = scale(lookup(emit_low[c], c)).astype(jnp.bfloat16)
        scaled_low[c] = scaled
        linear = dot(trans_low[c], scaled, 1, 0)
        linear_full[...] = linear
        linear_low[c] = linear_full[quarter_of(part), :]
        weight = jnp.where(parent_low[leaf * low_count + c] == me, 1.0, 0.0)
        inside_own[...] += weight * jnp.log(linear)
        return carry

    first = low_count * 7 // 10
    lax.fori_loop(0, first, near, 0)

    wait_recv(far_up.at[:, pl.ds(0, states - rows)], 3)

    def sum_far(t):
        total = jnp.zeros((rows, images * parts), jnp.float32)
        for l in range(leaves):
            for s in range(REMOTE):
                weight = jnp.where(far_parent[l * REMOTE + s] == t, 1.0, 0.0)
                total += weight * far_slices[l, s]
        return total

    def send_half(h, t, l, q):
        send(mid_send.at[h, t], mid_sums.at[h, slice_of(leaf, part)], 12 + h, l, q)

    def send_sum(t, l, q):
        total = sum_far(t)
        for h in range(HALVES):
            mid_send[h, t] = total[:, h * wide : (h + 1) * wide]
        send_half(0, t, l, q)

    each_other(send_sum)
    for h in range(1, HALVES):
        each_other(functools.partial(send_half, h))
    total = sum_far(me)
    for h in range(HALVES):
        mid_sums[h, slice_of(leaf, part), :] = total[:, h * wide : (h + 1) * wide]

    lax.fori_loop(first, low_count, near, 0)

    for h in range(HALVES):
        wait_recv(mid_sums.at[h, pl.ds(0, states - rows)], 12 + h)
        exact = scale(inside_own[:, lanes(h)] + mid_sums[h])
        post_mid[h] = exact
        scaled = exact.astype(jnp.bfloat16)
        scaled_mid[:, lanes(h)] = scaled
        linear = dot(trans_mid[...], scaled, 1, 0)
        linear_mid[h] = linear
        up_mid[h] = jnp.log(linear)
        each_other(
            lambda t, l, q: send(
                up_mid.at[h, slice_of(l, q)], up_slices.at[h, me], 14 + h, l, q
            )
        )
        up_slices[h, me] = up_mid[h, slice_of(leaf, part), :]

    wait_recv(own_top.at[pl.ds(0, states - rows)], 1)
    for h in range(HALVES):
        wait_recv(up_slices.at[h, pl.ds(0, devices - 1)], 14 + h)

        def top(r, carry):
            total = edge_top[r, :, lanes(h)]
            for p in range(devices):
                weight = jnp.where(parent_mid[p] == r, 1.0, 0.0)
                total += weight * up_slices[h, p]
            totals[h, r] = total
            return carry

        lax.fori_loop(0, leaves, top, 0)

        def send_total(t, l, q):
            total_send[h, t] = totals[h, parent_mid[t]]
            send(total_send.at[h, t], total_mine.at[h, slice_of(leaf, part)], 16 + h, l, q)

        each_other(send_total)
        total_mine[h, slice_of(leaf, part), :] = totals[h, parent_mid[me]]

    for h in range(HALVES):
        wait_recv(total_mine.at[h, pl.ds(0, states - rows)], 16 + h)
        reached = scale(total_mine[h])
        share = (
            reached / (linear_mid[h] * jnp.sum(reached, axis=0, keepdims=True))
        ).astype(jnp.bfloat16)
        share_mid[:, lanes(h)] = share
        posterior = post_mid[h] * dot(trans_mid[...], share, 0, 0)
        post_mid[h] = posterior / jnp.sum(posterior, axis=0, keepdims=True)
        each_other(
            lambda t, l, q: send(
                post_mid.at[h, slice_of(l, q)], post_slices[h].at[me], 18 + h, l, q
            )
        )
        post_slices[h][me] = post_mid[h, slice_of(leaf, part), :]

    for h in range(HALVES):
        each_part(
            lambda q: send(
                post_mid.at[h, quarter_of(q)], post_near.at[part, :, lanes(h)], 20 + h, leaf, q
            )
        )
        post_near[part, :, lanes(h)] = post_mid[h, quarter_of(part), :]

    def finished(share, scaled, weight):
        counts = dot(share, scaled, 1, 1) * weight.astype(jnp.float32) + PSEUDO
        return states * counts / jnp.sum(counts, axis=-1, keepdims=True)

    counts_own[...] = finished(share_mid[...], scaled_mid[...], trans_mid[...])

    landing = pl.ds(pl.multiple_of(leaf * rows, rows), rows)
    for h in range(HALVES):
        wait_recv(post_slices[h].at[pl.ds(0, devices - 1)], 18 + h)

        def pick(l):
            for s in range(REMOTE):
                parent = jnp.maximum(far_parent[l * REMOTE + s], 0)
                post_send[h, l, s] = post_slices[h][parent]

        def send_pick(l):
            pick(l)
            send(
                post_send.at[h, l],
                post_far.at[:, landing, lanes(h)],
                22 + h,
                l,
                part,
            )

        each_leaf(send_pick)
        pick(leaf)
        post_far[:, landing, lanes(h)] = post_send[h, leaf]

    each_part(lambda q: send(counts_own.at[quarter_of(q)], counts_mid.at[part], 2, leaf, q))
    counts_mid[part] = counts_own[quarter_of(part), :]

    def update_of(c, found):
        share = (found / linear_low[c]).astype(jnp.bfloat16)
        return finished(share, scaled_low[c], trans_low[c, quarter_of(part), :])

    for h in range(HALVES):
        wait_recv(post_mid.at[h, pl.ds(0, states - share_rows)], 20 + h)

    def near_update(c, carry):
        update_low[c] = update_of(c, post_near[jnp.minimum(place[c], mid_count - 1)])
        return carry

    lax.fori_loop(0, low_count, near_update, 0)
    wait_recv(counts_mid.at[pl.ds(0, parts - 1)], 2)
    update_mid[...] = counts_mid[...]
    for h in range(HALVES):
        wait_recv(post_send.at[h, pl.ds(0, leaves - 1)], 22 + h)

    def far_update(s, carry):
        far_counts[s] = update_of(far_index[s], post_far[s])
        return carry

    lax.fori_loop(0, REMOTE, far_update, 0)

    def choose(c, carry):
        slot = place[c] - mid_count
        update_low[c] = jnp.where(
            slot >= 0, far_counts[jnp.maximum(slot, 0)], update_low[c]
        )
        return carry

    lax.fori_loop(0, low_count, choose, 0)

    wait_send(pix.at[pl.ds(0, parts - 1)], 0)
    wait_send(own_top.at[pl.ds(0, states - rows)], 1)
    wait_send(counts_mid.at[pl.ds(0, parts - 1)], 2)
    wait_send(far_up.at[:, pl.ds(0, states - rows)], 3)
    for h in range(HALVES):
        wait_send(mid_send.at[h, pl.ds(0, devices - 1)], 12 + h)
        wait_send(up_slices.at[h, pl.ds(0, devices - 1)], 14 + h)
        wait_send(total_send.at[h, pl.ds(0, devices - 1)], 16 + h)
        wait_send(post_slices[h].at[pl.ds(0, devices - 1)], 18 + h)
        wait_send(post_mid.at[h, pl.ds(0, states - share_rows)], 20 + h)
        wait_send(post_send.at[h, pl.ds(0, leaves - 1)], 22 + h)


def fused(
    leaves,
    parts,
    pixels_low,
    pixels_mid,
    pixels_top,
    emit_low,
    emit_mid,
    emit_top,
    trans_low,
    trans_mid,
    outside_top,
    parent_low,
    parent_mid,
):
    low_count, images = pixels_low.shape
    mid_count = pixels_mid.shape[0]
    states = trans_low.shape[2]
    devices = leaves * parts
    share_rows = states // parts
    rows = states // devices
    whole = images * parts
    wide = whole // HALVES
    held = -(-(low_count + mid_count) // 8) * 8
    real, half = jnp.float32, jnp.bfloat16
    vmem = pltpu.VMEM
    arrays = (pixels_low, pixels_mid, pixels_top, emit_low, emit_mid, emit_top, trans_low)
    arrays += (trans_mid, outside_top)
    return pl.pallas_call(
        functools.partial(kernel, leaves, parts),
        out_shape=(
            vmem((low_count, share_rows, states), real),
            vmem((mid_count, share_rows, states), real),
        ),
        in_specs=[pl.BlockSpec(memory_space=pltpu.SMEM)] * 2
        + [pl.BlockSpec(memory_space=pltpu.HBM)] * len(arrays),
        out_specs=(pl.BlockSpec(memory_space=pltpu.VMEM),) * 2,
        scratch_shapes=[
            pltpu.SMEM((REMOTE,), jnp.int32),
            pltpu.SMEM((leaves * REMOTE,), jnp.int32),
            pltpu.SMEM((low_count,), jnp.int32),
            vmem(pixels_low.shape, jnp.int32),
            vmem(pixels_mid.shape, jnp.int32),
            vmem(pixels_top.shape, jnp.int32),
            vmem(emit_low.shape, half),
            vmem(emit_mid.shape[1:], half),
            vmem(emit_top.shape, half),
            vmem(trans_low.shape, half),
            vmem(trans_mid.shape[1:], half),
            vmem(outside_top.shape, real),
            vmem((parts, held, images), jnp.int32),
            vmem((leaves, rows, whole), real),
            vmem((states, images), real),
            vmem((REMOTE, states, images), real),
            vmem((leaves, REMOTE, rows, whole), real),
            vmem((HALVES, devices, rows, wide), real),
            vmem((HALVES, states, wide), real),
            vmem((states, whole), real),
            vmem((low_count, states, whole), half),
            vmem((low_count, share_rows, whole), real),
            vmem((states, whole), real),
            vmem((HALVES, states, wide), real),
            vmem((HALVES, devices, rows, wide), real),
            vmem((HALVES, leaves, rows, wide), real),
            vmem((HALVES, devices, rows, wide), real),
            vmem((HALVES, states, wide), real),
            vmem((states, whole), half),
            vmem((HALVES, states, wide), real),
            vmem((states, whole), half),
            vmem((HALVES, states, wide), real),
            (vmem((devices, rows, wide), real),) * HALVES,
            vmem((HALVES, leaves, REMOTE, rows, wide), real),
            vmem((mid_count, share_rows, whole), real),
            vmem((REMOTE, share_rows, whole), real),
            vmem((mid_count, share_rows, states), real),
            vmem((states, states), real),
            vmem((REMOTE, share_rows, states), real),
            pltpu.SemaphoreType.DMA((24,)),
            pltpu.SemaphoreType.DMA((24,)),
            pltpu.SemaphoreType.DMA((len(arrays),)),
        ],
        compiler_params=pltpu.CompilerParams(
            collective_id=0, has_side_effects=True, vmem_limit_bytes=62 * 2**20
        ),
    )(parent_low, parent_mid, *arrays)


def solution(mesh):
    leaves, parts = mesh.shape["leaf"], mesh.shape["batch"]
    fits = 256 % (8 * leaves * parts) == 0
    chosen = functools.partial(fused, leaves, parts) if fits else body
    return jax.shard_map(
        chosen,
        mesh=mesh,
        in_specs=(
            P("leaf", "batch"),
            P("leaf", "batch"),
            P("leaf", "batch"),
            P("leaf", None, None),
            P("leaf", None, None),
            P("leaf", None, None),
            P("leaf", None, None),
            P("leaf", None, None),
            P("leaf", "batch", None),
            P(),
            P(),
        ),
        out_specs=(P("leaf", "batch", None), P("leaf", "batch", None)),
        check_vma=False,
    )
```

```python
import functools

import jax
import jax.numpy as jnp
from jax import lax
from jax.experimental import pallas as pl
from jax.experimental.pallas import tpu as pltpu
from jax.sharding import PartitionSpec as P

PSEUDO = 0.001
REMOTE = 3
HALVES = 2
STRIDE = 13
MESH = pl.DeviceIdType.MESH


def lookup_all(table, pixels):
    levels = jnp.arange(table.shape[1], dtype=jnp.int32)
    picks = (pixels[:, :, None] == levels[None, None, :]).astype(jnp.bfloat16)
    return jnp.einsum("nbv,nvk->nbk", picks, table, preferred_element_type=jnp.float32)


def upward_all(inside, weight):
    top = jnp.max(inside, axis=-1, keepdims=True)
    scaled = jnp.exp(inside - top).astype(jnp.bfloat16)
    linear = jnp.einsum("nbj,nij->nbi", scaled, weight, preferred_element_type=jnp.float32)
    return (jnp.log(linear) + top, scaled)


def edge_all(above, weight, scaled):
    peak = jnp.max(above, axis=-1, keepdims=True)
    pushed = jnp.exp(above - peak).astype(jnp.bfloat16)
    reach = jnp.einsum("nbi,nij->nbj", pushed, weight, preferred_element_type=jnp.float32)
    total = jnp.sum(reach * scaled.astype(jnp.float32), axis=-1, keepdims=True)
    share = (pushed.astype(jnp.float32) / total).astype(jnp.bfloat16)
    counts = jnp.einsum("nbi,nbj->nij", share, scaled, preferred_element_type=jnp.float32)
    return (counts * weight.astype(jnp.float32), jnp.log(reach) + peak)


def finish(summed):
    counts = summed + PSEUDO
    return counts.shape[-1] * counts / jnp.sum(counts, axis=-1, keepdims=True)


def body(
    pixels_low,
    pixels_mid,
    pixels_top,
    emit_low,
    emit_mid,
    emit_top,
    trans_low,
    trans_mid,
    outside_top,
    parent_low,
    parent_mid,
):
    devices = lax.axis_size("leaf")
    mid_count = emit_mid.shape[0]
    top_count = emit_top.shape[0]
    up_low, scaled_low = upward_all(lookup_all(emit_low, pixels_low), trans_low)
    emis_mid = lookup_all(emit_mid, pixels_mid)
    emis_top = lookup_all(emit_top, pixels_top)
    moved = lax.all_to_all(up_low, "leaf", split_axis=1, concat_axis=0, tiled=True)
    gathered_mid = jax.ops.segment_sum(moved, parent_low, num_segments=mid_count * devices)
    sums_mid = lax.all_to_all(gathered_mid, "leaf", split_axis=0, concat_axis=1, tiled=True)
    inside_mid = emis_mid + sums_mid
    up_mid, scaled_mid = upward_all(inside_mid, trans_mid)
    moved_mid = lax.all_to_all(up_mid, "leaf", split_axis=1, concat_axis=0, tiled=True)
    gathered_top = jax.ops.segment_sum(moved_mid, parent_mid, num_segments=top_count * devices)
    sums_top = lax.all_to_all(gathered_top, "leaf", split_axis=0, concat_axis=1, tiled=True)
    total_top = emis_top + sums_top + outside_top
    spread_top = lax.all_to_all(total_top, "leaf", split_axis=1, concat_axis=0, tiled=True)
    picked = lax.all_to_all(spread_top[parent_mid], "leaf", split_axis=0, concat_axis=1, tiled=True)
    counts_mid, outside_mid = edge_all(picked - up_mid, trans_mid, scaled_mid)
    update_mid = finish(lax.psum_scatter(counts_mid, "batch", scatter_dimension=1, tiled=True))
    total_mid = inside_mid + outside_mid
    spread_mid = lax.all_to_all(total_mid, "leaf", split_axis=1, concat_axis=0, tiled=True)
    above_low = lax.all_to_all(
        spread_mid[parent_low], "leaf", split_axis=0, concat_axis=1, tiled=True
    )
    counts_low, unused = edge_all(above_low - up_low, trans_low, scaled_low)
    update_low = finish(lax.psum_scatter(counts_low, "batch", scatter_dimension=1, tiled=True))
    return (update_low, update_mid)


def dot(a, b, left, right):
    return lax.dot_general(
        a, b, (((left,), (right,)), ((), ())), preferred_element_type=jnp.float32
    )


def kernel(
    leaves,
    parts,
    parent_low,
    parent_mid,
    pixels_low_hbm,
    pixels_mid_hbm,
    pixels_top_hbm,
    emit_low_hbm,
    emit_mid_hbm,
    emit_top_hbm,
    trans_low_hbm,
    trans_mid_hbm,
    outside_top_hbm,
    update_low,
    update_mid,
    far_index,
    far_parent,
    place,
    pixels_low,
    pixels_mid,
    pixels_top,
    emit_low,
    emit_mid,
    emit_top,
    trans_low,
    trans_mid,
    outside_top,
    pix,
    edge_top,
    own_top,
    far_up,
    far_slices,
    mid_send,
    mid_sums,
    inside_own,
    scaled_low,
    linear_low,
    linear_full,
    up_mid,
    up_slices,
    partial_own,
    partial_far,
    totals,
    total_send,
    total_mine,
    scaled_mid,
    linear_mid,
    share_mid,
    post_mid,
    post_slices,
    post_send,
    post_near,
    post_far,
    counts_mid,
    counts_own,
    far_counts,
    send_sem,
    recv_sem,
    load_sem,
):
    leaf = lax.axis_index("leaf")
    part = lax.axis_index("batch")
    devices = leaves * parts
    me = leaf * parts + part
    low_count = pixels_low.shape[0]
    mid_count = pixels_mid.shape[0]
    images = pixels_low.shape[1]
    states = trans_low.shape[2]
    share_rows = states // parts
    rows = states // devices
    wide = images * parts // HALVES

    loads = [
        pltpu.make_async_copy(source, target, load_sem.at[i])
        for i, (source, target) in enumerate(
            (
                (pixels_low_hbm, pixels_low),
                (emit_low_hbm, emit_low),
                (trans_low_hbm, trans_low),
                (pixels_mid_hbm, pixels_mid),
                (pixels_top_hbm, pixels_top),
                (emit_top_hbm, emit_top),
                (outside_top_hbm, outside_top),
                (emit_mid_hbm.at[part], emit_mid),
                (trans_mid_hbm.at[part], trans_mid),
            )
        )
    ]
    for load in loads:
        load.start()

    def slice_of(l, q):
        return pl.ds(pl.multiple_of(q * share_rows + l * rows, rows), rows)

    def quarter_of(q):
        return pl.ds(pl.multiple_of(q * share_rows, share_rows), share_rows)

    side = leaves // 2
    pairs = devices // 2
    base = lax.div(leaf, side) * side
    spot = lax.rem(me, pairs)

    def tall_slice_of(l, q):
        start = q * share_rows + lax.rem(l, side) * (2 * rows)
        return pl.ds(pl.multiple_of(start, 2 * rows), 2 * rows)

    def each_near(step):
        def one(k, carry):
            t = lax.rem(spot + 5 * k, pairs)
            step(t, base + lax.div(t, parts), lax.rem(t, parts))
            return carry

        lax.fori_loop(1, pairs, one, 0)

    def lanes(h):
        return pl.ds(h * wide, wide)

    def send(src, dst, phase, l, q):
        pltpu.make_async_remote_copy(
            src_ref=src,
            dst_ref=dst,
            send_sem=send_sem.at[phase],
            recv_sem=recv_sem.at[phase],
            device_id=(l, q),
            device_id_type=MESH,
        ).start()

    def wait_recv(ref, phase):
        pltpu.make_async_copy(ref, ref, recv_sem.at[phase]).wait()

    def wait_send(ref, phase):
        pltpu.make_async_copy(ref, ref, send_sem.at[phase]).wait()

    def each_other(step):
        def one(k, carry):
            t = lax.rem(me + STRIDE * k, devices)
            step(t, lax.div(t, parts), lax.rem(t, parts))
            return carry

        lax.fori_loop(1, devices, one, 0)

    def each_leaf(step):
        def one(k, carry):
            step(lax.rem(leaf + 3 * k, leaves))
            return carry

        lax.fori_loop(1, leaves, one, 0)

    def each_part(step):
        def one(k, carry):
            step(lax.rem(part + k, parts))
            return carry

        lax.fori_loop(1, parts, one, 0)

    barrier = pltpu.get_barrier_semaphore()

    def greet(t, l, q):
        pl.semaphore_signal(barrier, inc=1, device_id=(l, q), device_id_type=MESH)

    each_other(greet)

    def far_row(l, carry):
        found = jnp.int32(0)
        parents = [jnp.int32(-1)] * REMOTE
        for c in range(low_count):
            parent = parent_low[l * low_count + c]
            away = lax.div(parent, mid_count) != l
            for s in range(REMOTE):
                parents[s] = jnp.where(away & (found == s), parent, parents[s])
            found = found + jnp.where(away, 1, 0)
        for s in range(REMOTE):
            far_parent[l * REMOTE + s] = parents[s]
        return carry

    lax.fori_loop(0, leaves, far_row, 0)
    found = jnp.int32(0)
    nodes = [jnp.int32(0)] * REMOTE
    for c in range(low_count):
        parent = parent_low[leaf * low_count + c]
        away = lax.div(parent, mid_count) != leaf
        for s in range(REMOTE):
            nodes[s] = jnp.where(away & (found == s), c, nodes[s])
        place[c] = jnp.where(
            away, mid_count + jnp.minimum(found, REMOTE - 1), lax.rem(parent, mid_count)
        )
        found = found + jnp.where(away, 1, 0)
    for s in range(REMOTE):
        far_index[s] = nodes[s]

    levels = lax.broadcasted_iota(jnp.int32, (emit_low.shape[1], images), 0)

    def picks(row):
        return jnp.where(levels == row, 1.0, 0.0).astype(jnp.bfloat16)

    def scale(inside):
        return jnp.exp(inside - jnp.max(inside, axis=0, keepdims=True))

    for load in loads[0:3]:
        load.wait()

    def message(node):
        inside = dot(emit_low[node], picks(pixels_low[pl.ds(node, 1), :]), 0, 0)
        scaled = scale(inside).astype(jnp.bfloat16)
        return jnp.log(dot(trans_low[node], scaled, 1, 0))

    def far(s, carry):
        far_up[s] = message(far_index[s])
        return carry

    lax.fori_loop(0, REMOTE, far, 0)
    mine = pl.ds(pl.multiple_of(part * images, images), images)
    loads[3].wait()
    pix[part, 0:low_count, :] = pixels_low[...]
    pix[part, low_count : low_count + mid_count, :] = pixels_mid[...]
    pl.semaphore_wait(barrier, devices - 1)
    each_part(lambda q: send(pix.at[part], pix.at[part], 0, leaf, q))
    each_other(
        lambda t, l, q: send(
            far_up.at[:, slice_of(l, q), :], far_slices.at[leaf, :, :, mine], 3, l, q
        )
    )
    far_slices[leaf, :, :, mine] = far_up[:, slice_of(leaf, part), :]
    for load in loads[4:7]:
        load.wait()
    own_top[...] = dot(emit_top[0], picks(pixels_top[...]), 0, 0) + outside_top[0].T
    each_near(
        lambda t, l, q: send(
            own_top.at[tall_slice_of(l, q)],
            edge_top.at[lax.rem(leaf, side), :, mine],
            1,
            l,
            q,
        )
    )
    edge_top[lax.rem(leaf, side), :, mine] = own_top[tall_slice_of(leaf, part), :]
    wait_recv(pix.at[pl.ds(0, parts - 1)], 0)

    def lookup(table, node):
        chosen = jnp.concatenate(
            [picks(pix[q, pl.ds(node, 1), :]) for q in range(parts)], axis=1
        )
        return dot(table, chosen, 0, 0)

    loads[7].wait()
    loads[8].wait()
    inside_own[...] = lookup(emit_mid[...], low_count + part)

    def near(c, carry):
        scaled = scale(lookup(emit_low[c], c)).astype(jnp.bfloat16)
        scaled_low[c] = scaled
        linear = dot(trans_low[c], scaled, 1, 0)
        linear_full[...] = linear
        linear_low[c] = linear_full[quarter_of(part), :]
        weight = jnp.where(parent_low[leaf * low_count + c] == me, 1.0, 0.0)
        inside_own[...] += weight * jnp.log(linear)
        return carry

    first = low_count * 7 // 10
    lax.fori_loop(0, first, near, 0)

    wait_recv(far_up.at[:, pl.ds(0, states - rows)], 3)

    def sum_far(t):
        total = jnp.zeros((rows, images * parts), jnp.float32)
        for l in range(leaves):
            for s in range(REMOTE):
                weight = jnp.where(far_parent[l * REMOTE + s] == t, 1.0, 0.0)
                total += weight * far_slices[l, s]
        return total

    def send_half(h, t, l, q):
        send(mid_send.at[h, t], mid_sums.at[h, slice_of(leaf, part)], 12 + h, l, q)

    def send_sum(t, l, q):
        total = sum_far(t)
        for h in range(HALVES):
            mid_send[h, t] = total[:, h * wide : (h + 1) * wide]
        send_half(0, t, l, q)

    each_other(send_sum)
    for h in range(1, HALVES):
        each_other(functools.partial(send_half, h))
    total = sum_far(me)
    for h in range(HALVES):
        mid_sums[h, slice_of(leaf, part), :] = total[:, h * wide : (h + 1) * wide]

    lax.fori_loop(first, low_count, near, 0)

    for h in range(HALVES):
        wait_recv(mid_sums.at[h, pl.ds(0, states - rows)], 12 + h)
        exact = scale(inside_own[:, lanes(h)] + mid_sums[h])
        post_mid[h] = exact
        scaled = exact.astype(jnp.bfloat16)
        scaled_mid[:, lanes(h)] = scaled
        linear = dot(trans_mid[...], scaled, 1, 0)
        linear_mid[h] = linear
        up_mid[h] = jnp.log(linear)
        each_near(
            lambda t, l, q: send(
                up_mid.at[h, tall_slice_of(l, q)], up_slices.at[h, spot], 14 + h, l, q
            )
        )
        up_slices[h, spot] = up_mid[h, tall_slice_of(leaf, part), :]

    wait_recv(own_top.at[pl.ds(0, states - 2 * rows)], 1)
    for h in range(HALVES):
        wait_recv(up_slices.at[h, pl.ds(0, pairs - 1)], 14 + h)

        def top(r, carry):
            here = jnp.where(lax.div(r, side) == lax.div(leaf, side), 1.0, 0.0)
            total = here * edge_top[lax.rem(r, side), :, lanes(h)]
            for p in range(pairs):
                weight = jnp.where(parent_mid[base * parts + p] == r, 1.0, 0.0)
                total += weight * up_slices[h, p]
            partial_own[h, r] = total
            return carry

        lax.fori_loop(0, leaves, top, 0)
        send(partial_own.at[h], partial_far.at[h], 24 + h, lax.rem(leaf + side, leaves), part)

    for h in range(HALVES):
        wait_recv(partial_far.at[h], 24 + h)
        totals[h] = partial_own[h] + partial_far[h]

        def send_total(t, l, q):
            total_send[h, t] = totals[h, parent_mid[base * parts + t]]
            send(
                total_send.at[h, t], total_mine.at[h, tall_slice_of(leaf, part)], 16 + h, l, q
            )

        each_near(send_total)
        total_mine[h, tall_slice_of(leaf, part), :] = totals[h, parent_mid[me]]

    for h in range(HALVES):
        wait_recv(total_mine.at[h, pl.ds(0, states - 2 * rows)], 16 + h)
        reached = scale(total_mine[h])
        share = (
            reached / (linear_mid[h] * jnp.sum(reached, axis=0, keepdims=True))
        ).astype(jnp.bfloat16)
        share_mid[:, lanes(h)] = share
        posterior = post_mid[h] * dot(trans_mid[...], share, 0, 0)
        post_mid[h] = posterior / jnp.sum(posterior, axis=0, keepdims=True)
        each_other(
            lambda t, l, q: send(
                post_mid.at[h, slice_of(l, q)], post_slices[h].at[me], 18 + h, l, q
            )
        )
        post_slices[h][me] = post_mid[h, slice_of(leaf, part), :]

    for h in range(HALVES):
        each_part(
            lambda q: send(
                post_mid.at[h, quarter_of(q)], post_near.at[part, :, lanes(h)], 20 + h, leaf, q
            )
        )
        post_near[part, :, lanes(h)] = post_mid[h, quarter_of(part), :]

    def finished(share, scaled, weight):
        counts = dot(share, scaled, 1, 1) * weight.astype(jnp.float32) + PSEUDO
        return states * counts / jnp.sum(counts, axis=-1, keepdims=True)

    counts_own[...] = finished(share_mid[...], scaled_mid[...], trans_mid[...])

    landing = pl.ds(pl.multiple_of(leaf * rows, rows), rows)
    for h in range(HALVES):
        wait_recv(post_slices[h].at[pl.ds(0, devices - 1)], 18 + h)

        def pick(l):
            for s in range(REMOTE):
                parent = jnp.maximum(far_parent[l * REMOTE + s], 0)
                post_send[h, l, s] = post_slices[h][parent]

        def send_pick(l):
            pick(l)
            send(
                post_send.at[h, l],
                post_far.at[:, landing, lanes(h)],
                22 + h,
                l,
                part,
            )

        each_leaf(send_pick)
        pick(leaf)
        post_far[:, landing, lanes(h)] = post_send[h, leaf]

    each_part(lambda q: send(counts_own.at[quarter_of(q)], counts_mid.at[part], 2, leaf, q))
    counts_mid[part] = counts_own[quarter_of(part), :]

    def update_of(c, found):
        share = (found / linear_low[c]).astype(jnp.bfloat16)
        return finished(share, scaled_low[c], trans_low[c, quarter_of(part), :])

    for h in range(HALVES):
        wait_recv(post_mid.at[h, pl.ds(0, states - share_rows)], 20 + h)

    def near_update(c, carry):
        update_low[c] = update_of(c, post_near[jnp.minimum(place[c], mid_count - 1)])
        return carry

    lax.fori_loop(0, low_count, near_update, 0)
    wait_recv(counts_mid.at[pl.ds(0, parts - 1)], 2)
    update_mid[...] = counts_mid[...]
    for h in range(HALVES):
        wait_recv(post_send.at[h, pl.ds(0, leaves - 1)], 22 + h)

    def far_update(s, carry):
        far_counts[s] = update_of(far_index[s], post_far[s])
        return carry

    lax.fori_loop(0, REMOTE, far_update, 0)

    def choose(c, carry):
        slot = place[c] - mid_count
        update_low[c] = jnp.where(
            slot >= 0, far_counts[jnp.maximum(slot, 0)], update_low[c]
        )
        return carry

    lax.fori_loop(0, low_count, choose, 0)

    wait_send(pix.at[pl.ds(0, parts - 1)], 0)
    wait_send(own_top.at[pl.ds(0, states - 2 * rows)], 1)
    wait_send(counts_mid.at[pl.ds(0, parts - 1)], 2)
    wait_send(far_up.at[:, pl.ds(0, states - rows)], 3)
    for h in range(HALVES):
        wait_send(mid_send.at[h, pl.ds(0, devices - 1)], 12 + h)
        wait_send(up_slices.at[h, pl.ds(0, pairs - 1)], 14 + h)
        wait_send(total_send.at[h, pl.ds(0, pairs - 1)], 16 + h)
        wait_send(partial_own.at[h], 24 + h)
        wait_send(post_slices[h].at[pl.ds(0, devices - 1)], 18 + h)
        wait_send(post_mid.at[h, pl.ds(0, states - share_rows)], 20 + h)
        wait_send(post_send.at[h, pl.ds(0, leaves - 1)], 22 + h)


def fused(
    leaves,
    parts,
    pixels_low,
    pixels_mid,
    pixels_top,
    emit_low,
    emit_mid,
    emit_top,
    trans_low,
    trans_mid,
    outside_top,
    parent_low,
    parent_mid,
):
    low_count, images = pixels_low.shape
    mid_count = pixels_mid.shape[0]
    states = trans_low.shape[2]
    devices = leaves * parts
    share_rows = states // parts
    rows = states // devices
    whole = images * parts
    wide = whole // HALVES
    held = -(-(low_count + mid_count) // 8) * 8
    real, half = jnp.float32, jnp.bfloat16
    vmem = pltpu.VMEM
    arrays = (pixels_low, pixels_mid, pixels_top, emit_low, emit_mid, emit_top, trans_low)
    arrays += (trans_mid, outside_top)
    return pl.pallas_call(
        functools.partial(kernel, leaves, parts),
        out_shape=(
            vmem((low_count, share_rows, states), real),
            vmem((mid_count, share_rows, states), real),
        ),
        in_specs=[pl.BlockSpec(memory_space=pltpu.SMEM)] * 2
        + [pl.BlockSpec(memory_space=pltpu.HBM)] * len(arrays),
        out_specs=(pl.BlockSpec(memory_space=pltpu.VMEM),) * 2,
        scratch_shapes=[
            pltpu.SMEM((REMOTE,), jnp.int32),
            pltpu.SMEM((leaves * REMOTE,), jnp.int32),
            pltpu.SMEM((low_count,), jnp.int32),
            vmem(pixels_low.shape, jnp.int32),
            vmem(pixels_mid.shape, jnp.int32),
            vmem(pixels_top.shape, jnp.int32),
            vmem(emit_low.shape, half),
            vmem(emit_mid.shape[1:], half),
            vmem(emit_top.shape, half),
            vmem(trans_low.shape, half),
            vmem(trans_mid.shape[1:], half),
            vmem(outside_top.shape, real),
            vmem((parts, held, images), jnp.int32),
            vmem((leaves // 2, 2 * rows, whole), real),
            vmem((states, images), real),
            vmem((REMOTE, states, images), real),
            vmem((leaves, REMOTE, rows, whole), real),
            vmem((HALVES, devices, rows, wide), real),
            vmem((HALVES, states, wide), real),
            vmem((states, whole), real),
            vmem((low_count, states, whole), half),
            vmem((low_count, share_rows, whole), real),
            vmem((states, whole), real),
            vmem((HALVES, states, wide), real),
            vmem((HALVES, devices // 2, 2 * rows, wide), real),
            vmem((HALVES, leaves, 2 * rows, wide), real),
            vmem((HALVES, leaves, 2 * rows, wide), real),
            vmem((HALVES, leaves, 2 * rows, wide), real),
            vmem((HALVES, devices // 2, 2 * rows, wide), real),
            vmem((HALVES, states, wide), real),
            vmem((states, whole), half),
            vmem((HALVES, states, wide), real),
            vmem((states, whole), half),
            vmem((HALVES, states, wide), real),
            (vmem((devices, rows, wide), real),) * HALVES,
            vmem((HALVES, leaves, REMOTE, rows, wide), real),
            vmem((mid_count, share_rows, whole), real),
            vmem((REMOTE, share_rows, whole), real),
            vmem((mid_count, share_rows, states), real),
            vmem((states, states), real),
            vmem((REMOTE, share_rows, states), real),
            pltpu.SemaphoreType.DMA((26,)),
            pltpu.SemaphoreType.DMA((26,)),
            pltpu.SemaphoreType.DMA((len(arrays),)),
        ],
        compiler_params=pltpu.CompilerParams(
            collective_id=0, has_side_effects=True, vmem_limit_bytes=62 * 2**20
        ),
    )(parent_low, parent_mid, *arrays)


def solution(mesh):
    leaves, parts = mesh.shape["leaf"], mesh.shape["batch"]
    fits = leaves % 2 == 0 and 256 % (8 * leaves * parts) == 0
    chosen = functools.partial(fused, leaves, parts) if fits else body
    return jax.shard_map(
        chosen,
        mesh=mesh,
        in_specs=(
            P("leaf", "batch"),
            P("leaf", "batch"),
            P("leaf", "batch"),
            P("leaf", None, None),
            P("leaf", None, None),
            P("leaf", None, None),
            P("leaf", None, None),
            P("leaf", None, None),
            P("leaf", "batch", None),
            P(),
            P(),
        ),
        out_specs=(P("leaf", "batch", None), P("leaf", "batch", None)),
        check_vma=False,
    )
```
